128 devices in a mesh: section: 2 (over x_hi), row: 8 (over y, core), col: 8 (over z, x_lo).
Axes of the slice: x: 4 (x_hi: 2, x_lo: 2; x = x_hi * 2 + x_lo), y: 4, z: 4, core: 2. Of those that a mesh axis runs over, the one named last changes fastest.
Arguments:
- layer_input: bfloat16 [2, 2, 128, 8192], P('section', None, 'col', 'row'), may hold values from -6 to 6
- top_grad: bfloat16 [2, 128, 8192], P(None, 'col', 'row'), may hold values from -6 to 6
- gate_weight: bfloat16 [2, 8192, 14336], P('section', 'row', 'col'), may hold values from -0.0625 to 0.0625
- up_weight: bfloat16 [2, 8192, 14336], P('section', 'row', 'col'), may hold values from -0.0625 to 0.0625
- down_weight: bfloat16 [2, 14336, 8192], P('section', 'col', 'row'), may hold values from -0.046875 to 0.046875
- activity: int32 [2, 2, 2, 8, 14], P('section', None, None, 'col'), may hold values from 0 to 28, as said below
Outputs:
- sent_grad: bfloat16 [2, 2, 128, 8192], P('section', None, 'col', 'row')
- gate_grad: bfloat16 [2, 8192, 14336], P('section', 'row', 'col')
- up_grad: bfloat16 [2, 8192, 14336], P('section', 'row', 'col')
- down_grad: bfloat16 [2, 14336, 8192], P('section', 'col', 'row')
The draws below stay inside these ranges and needn't reach their ends.
Inputs may be any that keep to these rules, and one draw needn't show every extreme that they name: `activity`: each list names distinct blocks below 28, then the value 28 marks empty slots up to the end; every list holds at least 3 blocks, and in every token block some column's list is full.
All inputs are finite; a program needn't handle non-finite values.
Results may differ from the reference program's by a relative error of at most 0.006.
Values may be sent and summed in bfloat16 or wider, within the bound.
A program may use at most 192 MiB of HBM per device.

```python
import jax
import jax.numpy as jnp

D = 8192
FF = 14336
BLK = 64
TB = 64
TOK = 128
MICRO = 2
LAYERS = 2
TBLK = 2
NBC = 28
KACT = 14
N_COL = 8


def draw_activity(key, part):
    row_total = LAYERS * MICRO * TBLK * N_COL
    row_keys = jax.random.split(jax.random.fold_in(key, 7), row_total)
    orders = jax.vmap(lambda one_key: jax.random.permutation(one_key, NBC))(row_keys)[:, :KACT]
    counts = jax.random.randint(jax.random.fold_in(key, 9), (row_total,), max(1, KACT // 4), KACT + 1)
    row_index = jnp.arange(row_total, dtype=jnp.int32)
    column = row_index % N_COL
    group = row_index // N_COL
    counts = jnp.where(column == group % N_COL, KACT, counts)
    slot_index = jnp.arange(KACT, dtype=jnp.int32)
    lists = jnp.where(slot_index[None, :] < counts[:, None], orders.astype(jnp.int32), NBC)
    return lists.astype(jnp.int32).reshape(LAYERS, MICRO, TBLK, N_COL, KACT)


def block_levels(rng, extent, shards, least, largest):
    def one(position, shards_of):
        steps = jax.random.uniform(jax.random.fold_in(jax.random.fold_in(rng, 6), position), (shards_of,), jnp.float32, least / len(shards), largest / len(shards))
        return jnp.repeat(jnp.exp(steps), extent[position] // shards_of).reshape((-1,) + (1,) * (len(extent) - position - 1))

    factor_of = one(*shards[0])
    for cut in shards[1:]:
        factor_of = factor_of * one(*cut)
    return factor_of


def noise(key, shape, width, bound, cuts=(), held_as=jnp.bfloat16):
    level = block_levels(key, shape, cuts, -0.22, 0.18) if cuts else 1.0
    result = jax.random.normal(key, shape, jnp.float32) * width * level
    return jnp.minimum(jnp.maximum(result, -bound), bound).astype(held_as)


def setup_inputs(seed: int = 0) -> dict:
    seeds = jax.random.split(jax.random.key(seed), 7)
    layer_input = noise(seeds[0], (LAYERS, MICRO, TOK, D), 1.0, 6.0, ((0, 2), (2, 8), (3, 8)))
    top_grad = noise(seeds[1], (MICRO, TOK, D), 1.0, 6.0, ((1, 8), (2, 8)))
    gate_weight = noise(seeds[2], (LAYERS, D, FF), D ** -0.5, 0.0625, ((0, 2), (1, 8), (2, 8)))
    up_weight = noise(seeds[3], (LAYERS, D, FF), D ** -0.5, 0.0625, ((0, 2), (1, 8), (2, 8)))
    down_weight = noise(seeds[4], (LAYERS, FF, D), FF ** -0.5, 0.046875, ((0, 2), (1, 8), (2, 8)))
    activity = draw_activity(jax.random.fold_in(seeds[6], 71), 0)
    return {"layer_input": layer_input, "top_grad": top_grad, "gate_weight": gate_weight, "up_weight": up_weight, "down_weight": down_weight, "activity": activity}


def block_mask(lists):
    blocks = jnp.arange(NBC, dtype=jnp.int32)
    block_on = jnp.any(lists[..., None] == blocks, axis=-2).astype(jnp.float32)
    spread = jnp.broadcast_to(block_on[:, None, :, :, None], (TBLK, TB, N_COL, NBC, BLK))
    return spread.reshape(TBLK * TB, N_COL * NBC * BLK)


def activate(gate_total, up_total, grad_total, keep_mask):
    positive = jnp.maximum(gate_total, 0.0)
    squared = keep_mask * positive * positive
    hidden = (squared * up_total).astype(jnp.bfloat16)
    grad_up = (squared * grad_total).astype(jnp.bfloat16)
    grad_hgate = (keep_mask * 2.0 * positive * up_total * grad_total).astype(jnp.bfloat16)
    return hidden, grad_hgate, grad_up


def layer_back(layer_in, grad_out, w_gate, w_up, w_down, lists):
    keep_mask = block_mask(lists)
    gate_total = jnp.dot(layer_in, w_gate, preferred_element_type=jnp.float32)
    up_total = jnp.dot(layer_in, w_up, preferred_element_type=jnp.float32)
    grad_total = jnp.dot(grad_out, w_down.T, preferred_element_type=jnp.float32)
    hidden, grad_hgate, grad_up = activate(gate_total, up_total, grad_total, keep_mask)
    down_term = jnp.dot(hidden.T, grad_out, preferred_element_type=jnp.float32)
    gate_term = jnp.dot(layer_in.T, grad_hgate, preferred_element_type=jnp.float32)
    up_term = jnp.dot(layer_in.T, grad_up, preferred_element_type=jnp.float32)
    handed = grad_out.astype(jnp.float32) + jnp.dot(grad_hgate, w_gate.T, preferred_element_type=jnp.float32)
    handed = handed + jnp.dot(grad_up, w_up.T, preferred_element_type=jnp.float32)
    return handed.astype(jnp.bfloat16), gate_term, up_term, down_term


def reference(layer_input, top_grad, gate_weight, up_weight, down_weight, activity):
    sent_layers = [None] * LAYERS
    gate_list = [None] * LAYERS
    up_list = [None] * LAYERS
    down_list = [None] * LAYERS
    for layer_index in range(LAYERS - 1, -1, -1):
        sum_gate = jnp.zeros((D, FF), jnp.float32)
        sum_up = jnp.zeros((D, FF), jnp.float32)
        sum_down = jnp.zeros((FF, D), jnp.float32)
        handed_list = []
        for micro_index in range(MICRO):
            if layer_index == LAYERS - 1:
                grad_out = top_grad[micro_index]
            else:
                grad_out = sent_layers[layer_index + 1][micro_index]
            handed, gate_term, up_term, down_term = layer_back(
                layer_input[layer_index, micro_index], grad_out, gate_weight[layer_index],
                up_weight[layer_index], down_weight[layer_index], activity[layer_index, micro_index])
            sum_gate = sum_gate + gate_term
            sum_up = sum_up + up_term
            sum_down = sum_down + down_term
            handed_list.append(handed)
        sent_layers[layer_index] = jnp.stack(handed_list)
        gate_list[layer_index] = sum_gate.astype(jnp.bfloat16)
        up_list[layer_index] = sum_up.astype(jnp.bfloat16)
        down_list[layer_index] = sum_down.astype(jnp.bfloat16)
    return (jnp.stack(sent_layers), jnp.stack(gate_list), jnp.stack(up_list), jnp.stack(down_list))
```

```python
import functools

import jax
import jax.numpy as jnp
from jax import lax
from jax.experimental import pallas as pl
from jax.experimental.pallas import tpu as pltpu
from jax.sharding import PartitionSpec as P

MESH = pl.DeviceIdType.MESH
F32, BF16 = jnp.float32, jnp.bfloat16
NT = (((1,), (1,)), ((), ()))
TN = (((0,), (0,)), ((), ()))

BLK = 64
TOK = 128
DL = 1024
FL = 1792
NBLK = 28
SLOTS = 14
HALF = 7
COL_STEPS = ((1, 0), (3, 0), (2, 0), (0, 1), (1, 1), (3, 1), (2, 1))


def relay_kernel(
    x_hbm, top_hbm, wg_hbm, wu_hbm, wd_hbm, act_ref,
    sent_hbm, xall_hbm, dyall_hbm, hid_hbm, gh_hbm, gu_hbm,
    xs, dys, wg, wu, wd, dn, ps, pr, yo, ys, yr,
    agb0, agb1, agh0, agh1, hid, gh, gu, dxf, dxs, rr, sentv, inv_y, inv_i,
    w_sem, own_sem, out_sem,
    x_s, x_r, dy_s, dy_r, pair_s, pair_r, y_s, y_r,
    ag_s, ag_r, agp_s, agp_r, hg_s, hg_r, hgp_s, hgp_r, rs_s, rs_r, hand_s, hand_r,
):
    agb, agh = (agb0, agb1), (agh0, agh1)
    sec, row, col = (lax.axis_index(a) for a in ("section", "row", "col"))
    y, k = row // 2, lax.rem(row, 2)
    z, xl = col // 2, lax.rem(col, 2)
    last = sec == 1

    def at_col(step, sign=1):
        dz, dx = step
        zz = lax.rem(z + (dz if sign > 0 else 4 - dz), 4)
        return zz * 2 + ((1 - xl) if dx else xl)

    def col_dev(step, sign=1):
        return (sec, row, at_col(step, sign))

    def y_at(d):
        return lax.rem(y + d, 4)

    def y_dev(d):
        return (sec, y_at(d) * 2 + k, col)

    pair = (sec, 2 * y + 1 - k, col)
    relay = (1 - sec, row, 2 * z + 1 - xl)

    def remote(src, dst, ss, rs, dev):
        return pltpu.make_async_remote_copy(
            src_ref=src, dst_ref=dst, send_sem=ss, recv_sem=rs, device_id=dev, device_id_type=MESH
        )

    def rows16(c):
        return pl.ds(pl.multiple_of(c * 16, 16), 16)

    weights = [
        pltpu.make_async_copy(src.at[0], dst, w_sem.at[i])
        for i, (src, dst) in enumerate(((wg_hbm, wg), (wu_hbm, wu), (wd_hbm, wd)))
    ]
    own_x = [
        pltpu.make_async_copy(x_hbm.at[0, m], xs.at[m, rows16(col)], own_sem.at[m]) for m in range(2)
    ]
    own_dy = [
        pltpu.make_async_copy(top_hbm.at[m], dys.at[m, rows16(col)], own_sem.at[2 + m])
        for m in range(2)
    ]
    for c in own_x:
        c.start()

    @pl.when(last)
    def _():
        for c in own_dy:
            c.start()

    for c in weights:
        c.start()

    barrier = pltpu.get_barrier_semaphore()
    partners = [col_dev(s) for s in COL_STEPS] + [y_dev(d) for d in (1, 2, 3)] + [pair, relay]
    for dev in partners:
        pl.semaphore_signal(barrier, inc=1, device_id=dev, device_id_type=MESH)
    pl.semaphore_wait(barrier, len(partners))

    def send_x(m, i):
        return remote(x_hbm.at[0, m], xs.at[m, rows16(col)], x_s.at[m, i], x_r.at[m, i], col_dev(COL_STEPS[i]))

    def recv_x(m, i):
        block = xs.at[m, rows16(at_col(COL_STEPS[i], -1))]
        return remote(block, block, x_s.at[m, i], x_r.at[m, i], col_dev(COL_STEPS[i]))

    def dy_block(c):
        flipped = c + 1 - 2 * lax.rem(c, 2)
        return jnp.where(last, c, flipped)

    def send_dy(m, i, src):
        block = rows16(dy_block(col))
        return remote(src, dys.at[m, block], dy_s.at[m, i], dy_r.at[m, i], col_dev(COL_STEPS[i]))

    def recv_dy(m, i):
        block = dys.at[m, rows16(dy_block(at_col(COL_STEPS[i], -1)))]
        return remote(block, block, dy_s.at[m, i], dy_r.at[m, i], col_dev(COL_STEPS[i]))

    MATS = ((0, 2), (2, 1))

    def pair_copy(m, j):
        lo, n = MATS[j]
        return remote(
            ps.at[m, pl.ds(lo, n)], pr.at[m, pl.ds(lo, n)], pair_s.at[m, j], pair_r.at[m, j], pair
        )

    def y_copy(m, j, d):
        lo, n = MATS[j]
        return remote(
            ys.at[m, d - 1, pl.ds(lo, n)], yr.at[m, d - 1, pl.ds(lo, n)],
            y_s.at[m, j, d - 1], y_r.at[m, j, d - 1], y_dev(d),
        )

    def ag_y(buf, ss, rs, m, d):
        return remote(buf[m].at[y, k], buf[m].at[y, k], ss.at[m, d - 1], rs.at[m, d - 1], y_dev(d))

    def ag_y_recv(buf, ss, rs, m, d):
        block = buf[m].at[y_at(4 - d), k]
        return remote(block, block, ss.at[m, d - 1], rs.at[m, d - 1], y_dev(d))

    def ag_pair(buf, ss, rs, m, d):
        block = buf[m].at[y_at(4 - d) if d else y, k]
        return remote(block, block, ss.at[m, d], rs.at[m, d], pair)

    def ag_pair_recv(buf, ss, rs, m, d):
        block = buf[m].at[y_at(4 - d) if d else y, 1 - k]
        return remote(block, block, ss.at[m, d], rs.at[m, d], pair)

    def rs_copy(m, i):
        return remote(
            dxs.at[m, rows16(at_col(COL_STEPS[i]))], rr.at[m, i], rs_s.at[m, i], rs_r.at[m, i],
            col_dev(COL_STEPS[i]),
        )

    def hand_copy(m):
        return remote(sentv.at[m], dys.at[m, rows16(col)], hand_s.at[m], hand_r.at[m], relay)

    def hand_recv(m):
        block = dys.at[m, rows16(dy_block(col))]
        return remote(block, block, hand_s.at[m], hand_r.at[m], relay)

    outs = [
        (xs, xall_hbm), (dys, dyall_hbm), (hid, hid_hbm), (gh, gh_hbm), (gu, gu_hbm), (sentv, sent_hbm)
    ]

    def out_copy(j, m):
        src, dst = outs[j]
        if j == 5:
            return pltpu.make_async_copy(src.at[m], dst.at[0, m], out_sem.at[j, m])
        return pltpu.make_async_copy(src.at[m], dst.at[m], out_sem.at[j, m])

    left = lax.broadcasted_iota(jnp.int32, (32, 128), 1) < 64
    left16 = lax.broadcasted_iota(jnp.int32, (16, 128), 1) < 64

    def lay_out(acc, m, mat, j):
        for tb in range(2):
            for h in range(2):
                lo = acc[64 * tb : 64 * tb + 32, 128 * h : 128 * h + 128]
                hi = acc[64 * tb + 32 : 64 * tb + 64, 128 * h : 128 * h + 128]
                dn[m, mat, tb, 4 * j + 2 * h] = jnp.where(left, lo, pltpu.roll(hi, 64, 1))
                dn[m, mat, tb, 4 * j + 2 * h + 1] = jnp.where(left, pltpu.roll(lo, 64, 1), hi)

    def pack(m, mats):
        far = pl.ds(pl.multiple_of(16 * (1 - k), 16), 16)

        def body(i, _):
            for yy in range(4):
                tb, sh = yy // 2, yy % 2
                b = jnp.minimum(act_ref[0, m, tb, 0, sh * HALF + i], NBLK - 1)
                for mat in mats:
                    ps[m, mat, yy, i] = dn[m, mat, tb, b, far, :]
            return 0

        lax.fori_loop(0, HALF, body, 0)

    def gate_up(m):
        own_x[m].wait()
        for i in range(7):
            recv_x(m, i).wait_recv()
        if m == 0:
            weights[0].wait()
            weights[1].wait()
        out_copy(0, m).start()

        def body(j, _):
            cut = pl.ds(pl.multiple_of(j * 256, 256), 256)
            lay_out(jnp.dot(xs[m], wg[:, cut], preferred_element_type=F32), m, 0, j)
            lay_out(jnp.dot(xs[m], wu[:, cut], preferred_element_type=F32), m, 1, j)
            return 0

        lax.fori_loop(0, 7, body, 0)
        pack(m, (0, 1))
        pair_copy(m, 0).start()

    def back(m):
        if m == 0:
            weights[2].wait()
        for i in range(7):
            recv_dy(m, i).wait_recv()
        out_copy(1, m).start()

        def body(j, _):
            cut = pl.ds(pl.multiple_of(j * 256, 256), 256)
            lay_out(lax.dot_general(dys[m], wd[cut, :], NT, preferred_element_type=F32), m, 2, j)
            return 0

        lax.fori_loop(0, 7, body, 0)
        pack(m, (2,))
        pair_copy(m, 1).start()

    def reduce_pair(m, j):
        pair_copy(m, j).wait_recv()
        lo, n = MATS[j]
        near = pl.ds(pl.multiple_of(16 * k, 16), 16)
        for d in (2, 1, 3, 0):
            yy = y_at(d)
            tb, sh = yy // 2, lax.rem(yy, 2)

            def body(i, _):
                b = jnp.minimum(act_ref[0, m, tb, 0, sh * HALF + i], NBLK - 1)
                for mat in range(lo, lo + n):
                    total = dn[m, mat, tb, b, near, :] + pr[m, mat, yy, i]
                    if d:
                        ys[m, d - 1, mat, i] = total.astype(BF16)
                    else:
                        yo[m, mat, i] = total
                return 0

            lax.fori_loop(0, HALF, body, 0)
            if d:
                y_copy(m, j, d).start()

    def activate(m):
        for j in range(2):
            for d in (1, 2, 3):
                y_copy(m, j, d).wait_recv()

        def body(i, _):
            sums = []
            for mat in range(3):
                total = yo[m, mat, i]
                for d in range(3):
                    total = total + yr[m, d, mat, i].astype(F32)
                sums.append(total)
            gate, up, grad = sums
            r = jnp.maximum(gate, 0.0)
            sq = r * r
            agh[m][y, k, i] = (sq * up).astype(BF16)
            agb[m][y, k, 0, i] = (2.0 * r * up * grad).astype(BF16)
            agb[m][y, k, 1, i] = (sq * grad).astype(BF16)
            return 0

        lax.fori_loop(0, HALF, body, 0)
        for d in (2, 1, 3):
            ag_y(agb, ag_s, ag_r, m, d).start()
        ag_pair(agb, agp_s, agp_r, m, 0).start()
        for d in (2, 1, 3):
            ag_y(agh, hg_s, hg_r, m, d).start()
        ag_pair(agh, hgp_s, hgp_r, m, 0).start()

    def forward(buf, sems, m):
        ss, rs, pss, prs = sems
        for d in (1, 3, 2):
            ag_y_recv(buf, ss, rs, m, d).wait_recv()
            ag_pair(buf, pss, prs, m, d).start()

    def expand(m, tile_of, dst_of):
        def body(n, _):
            cut = pl.ds(pl.multiple_of(n * 128, 128), 128)
            for tb in range(2):
                ye, ie = inv_y[m, tb, 2 * n], inv_i[m, tb, 2 * n]
                yd, idd = inv_y[m, tb, 2 * n + 1], inv_i[m, tb, 2 * n + 1]
                for kk in range(2):
                    for src, dst in zip(tile_of, dst_of):
                        a = src(ye, kk, ie).astype(F32)
                        b = src(yd, kk, idd).astype(F32)
                        top = 64 * tb + 16 * kk
                        dst[m, top : top + 16, cut] = jnp.where(left16, a, pltpu.roll(b, 64, 1)).astype(BF16)
                        dst[m, top + 32 : top + 48, cut] = jnp.where(left16, pltpu.roll(a, 64, 1), b).astype(BF16)
            return 0

        lax.fori_loop(0, NBLK // 2, body, 0)

    def input_grad(m):
        for d in (0, 1, 3, 2):
            ag_pair_recv(agb, agp_s, agp_r, m, d).wait_recv()
        expand(
            m,
            (lambda a, b, c: agb[m][a, b, 0, c], lambda a, b, c: agb[m][a, b, 1, c]),
            (gh, gu),
        )

        def body(j, _):
            cut = pl.ds(pl.multiple_of(j * 256, 256), 256)
            part = lax.dot_general(gh[m], wg[cut, :], NT, preferred_element_type=F32)
            part = part + lax.dot_general(gu[m], wu[cut, :], NT, preferred_element_type=F32)
            dxf[m, :, cut] = part
            dxs[m, :, cut] = part.astype(BF16)
            return 0

        lax.fori_loop(0, 4, body, 0)
        for i in (6, 4, 5, 2, 3, 0, 1):
            rs_copy(m, i).start()
        out_copy(3, m).start()
        out_copy(4, m).start()

    def finish(m):
        for i in range(7):
            rs_copy(m, i).wait_recv()
        total = dys[m, rows16(col), :].astype(F32) + dxf[m, rows16(col), :]
        for i in range(7):
            total = total + rr[m, i].astype(F32)
        sentv[m] = total.astype(BF16)

        @pl.when(last)
        def _():
            hand_copy(m).start()

        out_copy(5, m).start()

    def hidden(m):
        forward(agh, (hg_s, hg_r, hgp_s, hgp_r), m)
        for d in range(4):
            ag_pair_recv(agh, hgp_s, hgp_r, m, d).wait_recv()
        expand(m, (lambda a, b, c: agh[m][a, b, c],), (hid,))
        out_copy(2, m).start()

    def take_dy(m):
        hand_recv(m).wait_recv()
        for i in (6, 4, 5, 2, 3, 0, 1):
            send_dy(m, i, dys.at[m, rows16(dy_block(col))]).start()

    def forward_grads(m):
        forward(agb, (ag_s, ag_r, agp_s, agp_r), m)

    order = (6, 4, 5, 2, 3, 0, 1)
    for m in range(2):
        for i in order:
            send_x(m, i).start()

        @pl.when(last)
        def _():
            for i in order:
                send_dy(m, i, top_hbm.at[m]).start()

    for m in range(2):
        agb[m][4] = jnp.zeros(agb[m].shape[1:], BF16)
        agh[m][4] = jnp.zeros(agh[m].shape[1:], BF16)
        for tb in range(2):
            def body(n, _):
                slot = jnp.int32(2 * SLOTS)
                for s in range(SLOTS):
                    slot = jnp.where(act_ref[0, m, tb, 0, s] == n, s, slot)
                inv_y[m, tb, n] = jnp.where(slot < SLOTS, 2 * tb + jnp.where(slot < HALF, 0, 1), 4)
                inv_i[m, tb, n] = jnp.where(
                    slot < SLOTS, jnp.where(slot < HALF, slot, slot - HALF), 0
                )
                return 0

            lax.fori_loop(0, NBLK, body, 0)

    @pl.when(last)
    def _():
        own_dy[0].wait()
        own_dy[1].wait()
        gate_up(0)
        back(0)
        reduce_pair(0, 0)
        reduce_pair(0, 1)
        gate_up(1)
        back(1)
        activate(0)
        reduce_pair(1, 0)
        reduce_pair(1, 1)
        forward_grads(0)
        input_grad(0)
        activate(1)
        forward_grads(1)
        finish(0)
        input_grad(1)
        hidden(0)
        hidden(1)
        finish(1)

    @pl.when(sec == 0)
    def _():
        gate_up(0)
        gate_up(1)
        reduce_pair(0, 0)
        reduce_pair(1, 0)
        take_dy(0)
        back(0)
        reduce_pair(0, 1)
        take_dy(1)
        activate(0)
        back(1)
        forward_grads(0)
        reduce_pair(1, 1)
        input_grad(0)
        activate(1)
        hidden(0)
        forward_grads(1)
        input_grad(1)
        finish(0)
        hidden(1)
        finish(1)

    for m in range(2):
        for i in range(7):
            send_x(m, i).wait_send()
            send_dy(m, i, dys.at[m, rows16(dy_block(col))]).wait_send()
            rs_copy(m, i).wait_send()
        for j in range(2):
            pair_copy(m, j).wait_send()
            for d in (1, 2, 3):
                y_copy(m, j, d).wait_send()
        for d in (1, 2, 3):
            ag_y(agb, ag_s, ag_r, m, d).wait_send()
            ag_y(agh, hg_s, hg_r, m, d).wait_send()
        for d in range(4):
            ag_pair(agb, agp_s, agp_r, m, d).wait_send()
            ag_pair(agh, hgp_s, hgp_r, m, d).wait_send()
        for j in range(6):
            out_copy(j, m).wait()

    @pl.when(last)
    def _():
        for m in range(2):
            hand_copy(m).wait_send()


def relay_call(layer_input, top_grad, gate_weight, up_weight, down_weight, activity):
    any_space = pl.BlockSpec(memory_space=pl.ANY)
    dma = pltpu.SemaphoreType.DMA
    vm = pltpu.VMEM
    tile = (HALF, 16, 128)
    return pl.pallas_call(
        relay_kernel,
        name="relay",
        out_shape=(
            jax.ShapeDtypeStruct((1, 2, 16, DL), BF16),
            jax.ShapeDtypeStruct((2, TOK, DL), BF16),
            jax.ShapeDtypeStruct((2, TOK, DL), BF16),
            jax.ShapeDtypeStruct((2, TOK, FL), BF16),
            jax.ShapeDtypeStruct((2, TOK, FL), BF16),
            jax.ShapeDtypeStruct((2, TOK, FL), BF16),
        ),
        in_specs=[any_space] * 5 + [pl.BlockSpec(memory_space=pltpu.SMEM)],
        out_specs=(any_space,) * 6,
        scratch_shapes=[
            vm((2, TOK, DL), BF16), vm((2, TOK, DL), BF16),
            vm((DL, FL), BF16), vm((DL, FL), BF16), vm((FL, DL), BF16),
            vm((2, 3, 2, NBLK, 32, 128), F32),
            vm((2, 3, 4) + tile, F32), vm((2, 3, 4) + tile, F32),
            vm((2, 3) + tile, F32), vm((2, 3, 3) + tile, BF16), vm((2, 3, 3) + tile, BF16),
            vm((5, 2, 2) + tile, BF16), vm((5, 2, 2) + tile, BF16),
            vm((5, 2) + tile, BF16), vm((5, 2) + tile, BF16),
            vm((2, TOK, FL), BF16), vm((2, TOK, FL), BF16), vm((2, TOK, FL), BF16),
            vm((2, TOK, DL), F32), vm((2, TOK, DL), BF16), vm((2, 7, 16, DL), BF16), vm((2, 16, DL), BF16),
            pltpu.SMEM((2, 2, NBLK), jnp.int32), pltpu.SMEM((2, 2, NBLK), jnp.int32),
            dma((3,)), dma((4,)), dma((6, 2)),
            dma((2, 7)), dma((2, 7)), dma((2, 7)), dma((2, 7)),
            dma((2, 2)), dma((2, 2)), dma((2, 2, 3)), dma((2, 2, 3)),
            dma((2, 3)), dma((2, 3)), dma((2, 4)), dma((2, 4)),
            dma((2, 3)), dma((2, 3)), dma((2, 4)), dma((2, 4)),
            dma((2, 7)), dma((2, 7)), dma((2,)), dma((2,)),
        ],
        compiler_params=pltpu.CompilerParams(
            collective_id=1, has_side_effects=True, vmem_limit_bytes=48 * 2**20
        ),
        cost_estimate=pl.CostEstimate(flops=5 * 2**30, bytes_accessed=16 * 2**20, transcendentals=0),
    )(layer_input, top_grad, gate_weight, up_weight, down_weight, activity)


def weights_kernel(x_ref, dy_ref, hid_ref, gh_ref, gu_ref, sent_ref, out_sent, og, ou, od, xt):
    @pl.when(pl.program_id(0) == 0)
    def _():
        xt[...] = x_ref[...].T
        out_sent[...] = sent_ref[...]

    og[0] = jnp.dot(xt[...], gh_ref[...], preferred_element_type=F32).astype(BF16)
    ou[0] = jnp.dot(xt[...], gu_ref[...], preferred_element_type=F32).astype(BF16)
    od[0] = lax.dot_general(hid_ref[...], dy_ref[...], TN, preferred_element_type=F32).astype(BF16)


def weights_call(x_all, dy_all, hid, gh, gu, sent):
    whole = lambda shape: pl.BlockSpec(shape, lambda j: (0,) * len(shape))
    cut = pl.BlockSpec((2 * TOK, 256), lambda j: (0, j))
    return pl.pallas_call(
        weights_kernel,
        name="weight_grads",
        grid=(FL // 256,),
        out_shape=(
            jax.ShapeDtypeStruct((1, 2, 16, DL), BF16),
            jax.ShapeDtypeStruct((1, DL, FL), BF16),
            jax.ShapeDtypeStruct((1, DL, FL), BF16),
            jax.ShapeDtypeStruct((1, FL, DL), BF16),
        ),
        in_specs=[whole((2 * TOK, DL)), whole((2 * TOK, DL)), cut, cut, cut, whole((1, 2, 16, DL))],
        out_specs=(
            whole((1, 2, 16, DL)),
            pl.BlockSpec((1, DL, 256), lambda j: (0, 0, j)),
            pl.BlockSpec((1, DL, 256), lambda j: (0, 0, j)),
            pl.BlockSpec((1, 256, DL), lambda j: (0, j, 0)),
        ),
        scratch_shapes=[pltpu.VMEM((DL, 2 * TOK), BF16)],
        compiler_params=pltpu.CompilerParams(
            dimension_semantics=("arbitrary",), vmem_limit_bytes=32 * 2**20
        ),
    )(x_all, dy_all, hid, gh, gu, sent)


def shards(layer_input, top_grad, gate_weight, up_weight, down_weight, activity):
    sent, x_all, dy_all, hid, gh, gu = relay_call(
        layer_input, top_grad, gate_weight, up_weight, down_weight, activity
    )
    flat = lambda a: a.reshape(2 * TOK, a.shape[-1])
    return weights_call(flat(x_all), flat(dy_all), flat(hid), flat(gh), flat(gu), sent)


def solution(mesh):
    in_specs = (
        P("section", None, "col", "row"),
        P(None, "col", "row"),
        P("section", "row", "col"),
        P("section", "row", "col"),
        P("section", "col", "row"),
        P("section", None, None, "col", None),
    )
    out_specs = (
        P("section", None, "col", "row"),
        P("section", "row", "col"),
        P("section", "row", "col"),
        P("section", "col", "row"),
    )
    return jax.shard_map(shards, mesh=mesh, in_specs=in_specs, out_specs=out_specs, check_vma=False)
```

```python
import functools

import jax
import jax.numpy as jnp
from jax import lax
from jax.experimental import pallas as pl
from jax.experimental.pallas import tpu as pltpu
from jax.sharding import PartitionSpec as P

MESH = pl.DeviceIdType.MESH
F32, BF16 = jnp.float32, jnp.bfloat16
NT = (((1,), (1,)), ((), ()))
TN = (((0,), (0,)), ((), ()))

BLK = 64
TOK = 128
DL = 1024
FL = 1792
NBLK = 28
SLOTS = 14
HALF = 7
COL_STEPS = ((1, 0), (3, 0), (2, 0), (0, 1), (1, 1), (3, 1), (2, 1))


def relay_kernel(
    plans,
    x_hbm, top_hbm, wg_hbm, wu_hbm, wd_hbm, act_hbm,
    sent_hbm, xall_hbm, dyall_hbm, hid_hbm, gh_hbm, gu_hbm,
    xs, dys, wg, wu, wd, wgt, wut, wdt, dn, ps, pr, yo, ys, yr,
    agb0, agb1, agh0, agh1, hid, gh, gu, dxf, dxs, rr, sentv, act_ref, inv_y, inv_i,
    w_sem, own_sem, out_sem,
    x_s, x_r, dy_s, dy_r, pair_s, pair_r, y_s, y_r,
    ag_s, ag_r, agp_s, agp_r, hg_s, hg_r, hgp_s, hgp_r, rs_s, rs_r, hand_s, hand_r,
):
    agb, agh = (agb0, agb1), (agh0, agh1)
    sec, row, col = (lax.axis_index(a) for a in ("section", "row", "col"))
    y, k = row // 2, lax.rem(row, 2)
    z, xl = col // 2, lax.rem(col, 2)
    last = sec == 1

    def at_col(step, sign=1):
        dz, dx = step
        zz = lax.rem(z + (dz if sign > 0 else 4 - dz), 4)
        return zz * 2 + ((1 - xl) if dx else xl)

    def col_dev(step, sign=1):
        return (sec, row, at_col(step, sign))

    def y_at(d):
        return lax.rem(y + d, 4)

    def y_dev(d):
        return (sec, y_at(d) * 2 + k, col)

    pair = (sec, 2 * y + 1 - k, col)
    relay = (1 - sec, row, 2 * z + 1 - xl)

    def remote(src, dst, ss, rs, dev):
        return pltpu.make_async_remote_copy(
            src_ref=src, dst_ref=dst, send_sem=ss, recv_sem=rs, device_id=dev, device_id_type=MESH
        )

    def rows16(c):
        return pl.ds(pl.multiple_of(c * 16, 16), 16)

    lists = pltpu.make_async_copy(act_hbm, act_ref, own_sem.at[4])
    weights = [
        pltpu.make_async_copy(src.at[0], dst, w_sem.at[i])
        for i, (src, dst) in enumerate(((wg_hbm, wg), (wu_hbm, wu), (wd_hbm, wd)))
    ]
    own_x = [
        pltpu.make_async_copy(x_hbm.at[0, m], xs.at[m, rows16(col)], own_sem.at[m]) for m in range(2)
    ]
    own_dy = [
        pltpu.make_async_copy(top_hbm.at[m], dys.at[m, rows16(col)], own_sem.at[2 + m])
        for m in range(2)
    ]
    lists.start()
    for c in own_x:
        c.start()
    for c in weights:
        c.start()

    barrier = pltpu.get_barrier_semaphore()
    partners = [col_dev(s) for s in COL_STEPS] + [y_dev(d) for d in (1, 2, 3)] + [pair, relay]
    for dev in partners:
        pl.semaphore_signal(barrier, inc=1, device_id=dev, device_id_type=MESH)
    pl.semaphore_wait(barrier, len(partners))

    def invert():
        lists.wait()
        for m in range(2):
            agb[m][4] = jnp.zeros(agb[m].shape[1:], BF16)
            agh[m][4] = jnp.zeros(agh[m].shape[1:], BF16)
            for tb in range(2):
                def body(n, _):
                    slot = jnp.int32(2 * SLOTS)
                    for s in range(SLOTS):
                        slot = jnp.where(act_ref[0, m, tb, 0, s] == n, s, slot)
                    inv_y[m, tb, n] = jnp.where(slot < SLOTS, 2 * tb + jnp.where(slot < HALF, 0, 1), 4)
                    inv_i[m, tb, n] = jnp.where(
                        slot < SLOTS, jnp.where(slot < HALF, slot, slot - HALF), 0
                    )
                    return 0

                lax.fori_loop(0, NBLK, body, 0)

    left = lax.broadcasted_iota(jnp.int32, (32, 128), 1) < 64
    left16 = lax.broadcasted_iota(jnp.int32, (16, 128), 1) < 64
    MATS = ((0, 2), (2, 1))
    far_first = (6, 4, 5, 2, 3, 0, 1)

    def run(is_last, plan, expected):
        sends, recvs, local = {}, {}, {}

        def start(key, src, dst, ss, rs, dev, landing=None):
            c = remote(src, dst, ss, rs, dev)
            c.start()
            sends[key] = c
            if landing is not None:
                recvs[key] = remote(landing, landing, ss, rs, dev)

        def arrived(*key):
            recvs.pop(key).wait_recv()

        local.update({("w", i): c for i, c in enumerate(weights)})
        local.update({("x", m): c for m, c in enumerate(own_x)})

        def start_local(key, src, dst, sem):
            c = pltpu.make_async_copy(src, dst, sem)
            c.start()
            local[key] = c

        def dy_block(c):
            return c if is_last else c + 1 - 2 * lax.rem(c, 2)

        def lay_out(acc, m, mat, j):
            for tb in range(2):
                for h in range(2):
                    lo = acc[64 * tb : 64 * tb + 32, 128 * h : 128 * h + 128]
                    hi = acc[64 * tb + 32 : 64 * tb + 64, 128 * h : 128 * h + 128]
                    dn[m, mat, tb, 4 * j + 2 * h] = jnp.where(left, lo, pltpu.roll(hi, 64, 1))
                    dn[m, mat, tb, 4 * j + 2 * h + 1] = jnp.where(left, pltpu.roll(lo, 64, 1), hi)

        def send_pair(m, j):
            lo, n = MATS[j]
            far = pl.ds(pl.multiple_of(16 * (1 - k), 16), 16)

            def body(i, _):
                for yy in range(4):
                    tb, sh = yy // 2, yy % 2
                    b = jnp.minimum(act_ref[0, m, tb, 0, sh * HALF + i], NBLK - 1)
                    for mat in range(lo, lo + n):
                        ps[m, mat, yy, i] = dn[m, mat, tb, b, far, :]
                return 0

            lax.fori_loop(0, HALF, body, 0, unroll=True)
            cut = pl.ds(lo, n)
            start(
                ("pair", m, j), ps.at[m, cut], pr.at[m, cut], pair_s.at[m, j], pair_r.at[m, j], pair,
                pr.at[m, cut],
            )

        def spread_x(m):
            for i in far_first:
                step = COL_STEPS[i]
                start(
                    ("x", m, i), x_hbm.at[0, m], xs.at[m, rows16(col)], x_s.at[m, i], x_r.at[m, i],
                    col_dev(step), xs.at[m, rows16(at_col(step, -1))],
                )

        def spread_top(m):
            own_dy[m].start()
            local["dy", m] = own_dy[m]
            spread_dy(m, top_hbm.at[m])

        def wait_x(m):
            local.pop(("x", m)).wait()
            for i in range(7):
                arrived("x", m, i)

        def spread_dy(m, src):
            block = rows16(dy_block(col))
            for i in far_first:
                step = COL_STEPS[i]
                start(
                    ("dy", m, i), src, dys.at[m, block], dy_s.at[m, i], dy_r.at[m, i],
                    col_dev(step), dys.at[m, rows16(dy_block(at_col(step, -1)))],
                )

        def take_dy(m):
            arrived("hand", m)
            spread_dy(m, dys.at[m, rows16(dy_block(col))])

        def gate_up(m):
            if m == 0:
                local.pop(("w", 0)).wait()
                local.pop(("w", 1)).wait()
            start_local((0, m), xs.at[m], xall_hbm.at[m], out_sem.at[0, m])

            def body(j, _):
                cut = pl.ds(pl.multiple_of(j * 256, 256), 256)
                lay_out(jnp.dot(xs[m], wg[:, cut], preferred_element_type=F32), m, 0, j)
                lay_out(jnp.dot(xs[m], wu[:, cut], preferred_element_type=F32), m, 1, j)
                return 0

            lax.fori_loop(0, 7, body, 0, unroll=True)
            send_pair(m, 0)

        def back(m):
            if is_last:
                local.pop(("dy", m)).wait()
            if ("w", 2) in local:
                local.pop(("w", 2)).wait()
            for i in range(7):
                arrived("dy", m, i)
            start_local((1, m), dys.at[m], dyall_hbm.at[m], out_sem.at[1, m])

            def body(j, _):
                cut = pl.ds(pl.multiple_of(j * 256, 256), 256)
                if is_last:
                    grad = lax.dot_general(dys[m], wd[cut, :], NT, preferred_element_type=F32)
                else:
                    grad = jnp.dot(dys[m], wdt[:, cut], preferred_element_type=F32)
                lay_out(grad, m, 2, j)
                return 0

            lax.fori_loop(0, 7, body, 0, unroll=True)
            send_pair(m, 1)

        def reduce_pair(m, j):
            arrived("pair", m, j)
            lo, n = MATS[j]
            near = pl.ds(pl.multiple_of(16 * k, 16), 16)
            cut = pl.ds(lo, n)
            for d in (2, 1, 3, 0):
                yy = y_at(d)
                tb, sh = yy // 2, lax.rem(yy, 2)

                def body(i, _):
                    b = jnp.minimum(act_ref[0, m, tb, 0, sh * HALF + i], NBLK - 1)
                    for mat in range(lo, lo + n):
                        total = dn[m, mat, tb, b, near, :] + pr[m, mat, yy, i]
                        if d:
                            ys[m, d - 1, mat, i] = total.astype(BF16)
                        else:
                            yo[m, mat, i] = total
                    return 0

                lax.fori_loop(0, HALF, body, 0, unroll=True)
                if d:
                    start(
                        ("y", m, j, d), ys.at[m, d - 1, cut], yr.at[m, d - 1, cut],
                        y_s.at[m, j, d - 1], y_r.at[m, j, d - 1], y_dev(d), yr.at[m, d - 1, cut],
                    )

        def spread(name, buf, m, sems):
            ss, rs, pss, prs = sems
            for d in (2, 1, 3):
                start(
                    (name, m, d), buf.at[y, k], buf.at[y, k], ss.at[m, d - 1], rs.at[m, d - 1], y_dev(d),
                    buf.at[y_at(4 - d), k],
                )
            start((name + "p", m, 0), buf.at[y, k], buf.at[y, k], pss.at[m, 0], prs.at[m, 0], pair, buf.at[y, 1 - k])

        def forward(name, buf, m, sems):
            ss, rs, pss, prs = sems
            for d in (1, 3, 2):
                arrived(name, m, d)
                yy = y_at(4 - d)
                start(
                    (name + "p", m, d), buf.at[yy, k], buf.at[yy, k], pss.at[m, d], prs.at[m, d], pair,
                    buf.at[yy, 1 - k],
                )

        grad_sems, hid_sems = (ag_s, ag_r, agp_s, agp_r), (hg_s, hg_r, hgp_s, hgp_r)

        def activate(m):
            for j in range(2):
                for d in (1, 2, 3):
                    arrived("y", m, j, d)

            def body(i, _):
                sums = []
                for mat in range(3):
                    total = yo[m, mat, i]
                    for d in range(3):
                        total = total + yr[m, d, mat, i].astype(F32)
                    sums.append(total)
                gate, up, grad = sums
                r = jnp.maximum(gate, 0.0)
                sq = r * r
                agh[m][y, k, i] = (sq * up).astype(BF16)
                agb[m][y, k, 0, i] = (2.0 * r * up * grad).astype(BF16)
                agb[m][y, k, 1, i] = (sq * grad).astype(BF16)
                return 0

            lax.fori_loop(0, HALF, body, 0, unroll=True)
            spread("g", agb[m], m, grad_sems)
            spread("h", agh[m], m, hid_sems)

        def forward_grads(m):
            forward("g", agb[m], m, grad_sems)

        def expand(m, sources, targets):
            def body(n, _):
                cut = pl.ds(pl.multiple_of(n * 128, 128), 128)
                for tb in range(2):
                    ya, ia = inv_y[m, tb, 2 * n], inv_i[m, tb, 2 * n]
                    yb, ib = inv_y[m, tb, 2 * n + 1], inv_i[m, tb, 2 * n + 1]
                    for kk in range(2):
                        for src, dst in zip(sources, targets):
                            a = src(ya, kk, ia).astype(F32)
                            b = src(yb, kk, ib).astype(F32)
                            top = 64 * tb + 16 * kk
                            dst[m, top : top + 16, cut] = jnp.where(left16, a, pltpu.roll(b, 64, 1)).astype(BF16)
                            dst[m, top + 32 : top + 48, cut] = jnp.where(left16, pltpu.roll(a, 64, 1), b).astype(BF16)
                return 0

            lax.fori_loop(0, NBLK // 2, body, 0, unroll=True)

        def expand_grads(m):
            for d in (0, 1, 3, 2):
                arrived("gp", m, d)
            expand(
                m, (lambda a, b, c: agb[m][a, b, 0, c], lambda a, b, c: agb[m][a, b, 1, c]), (gh, gu)
            )
            start_local((3, m), gh.at[m], gh_hbm.at[m], out_sem.at[3, m])
            start_local((4, m), gu.at[m], gu_hbm.at[m], out_sem.at[4, m])

        def input_grad(m):
            def body(j, half):
                cut = pl.ds(pl.multiple_of(j * 256, 256), 256)
                rows = pl.ds(pl.multiple_of(half * 512 + j * 256, 256), 256)
                if is_last:
                    part = lax.dot_general(gh[m], wg[rows, :], NT, preferred_element_type=F32)
                    part = part + lax.dot_general(gu[m], wu[rows, :], NT, preferred_element_type=F32)
                else:
                    part = jnp.dot(gh[m], wgt[:, rows], preferred_element_type=F32)
                    part = part + jnp.dot(gu[m], wut[:, rows], preferred_element_type=F32)
                dxf[m, half, :, cut] = part
                dxs[m, half, :, cut] = part.astype(BF16)

            for half in range(2):
                lax.fori_loop(0, 2, lambda j, c: (body(j, half), c)[1], 0, unroll=True)
                for i in far_first:
                    start(
                        ("rs", m, half, i), dxs.at[m, half, rows16(at_col(COL_STEPS[i]))], rr.at[m, half, i],
                        rs_s.at[m, half, i], rs_r.at[m, half, i], col_dev(COL_STEPS[i]), rr.at[m, half, i],
                    )

        def finish(m):
            for half in range(2):
                cols = slice(512 * half, 512 * half + 512)
                for i in range(7):
                    arrived("rs", m, half, i)
                total = dys[m, rows16(col), cols].astype(F32) + dxf[m, half, rows16(col), :]
                for i in range(7):
                    total = total + rr[m, half, i].astype(F32)
                sentv[m, :, cols] = total.astype(BF16)
            if is_last:
                start(("hand", m), sentv.at[m], dys.at[m, rows16(col)], hand_s.at[m], hand_r.at[m], relay)
            start_local((5, m), sentv.at[m], sent_hbm.at[0, m], out_sem.at[5, m])

        def turn():
            for i in range(3):
                if ("w", i) in local:
                    local.pop(("w", i)).wait()

            def body(j, _):
                cut = pl.ds(pl.multiple_of(j * 256, 256), 256)
                wgt[cut, :] = wg[:, cut].T
                wut[cut, :] = wu[:, cut].T
                wdt[:, cut] = wd[cut, :].T
                return 0

            lax.fori_loop(0, 7, body, 0)

        def hidden(m):
            forward("h", agh[m], m, hid_sems)
            for d in range(4):
                arrived("hp", m, d)
            expand(m, (lambda a, b, c: agh[m][a, b, c],), (hid,))
            start_local((2, m), hid.at[m], hid_hbm.at[m], out_sem.at[2, m])

        for m in expected:
            block = dys.at[m, rows16(dy_block(col))]
            recvs["hand", m] = remote(block, block, hand_s.at[m], hand_r.at[m], relay)
        table = dict(
            ax=spread_x, ady=spread_top, wx=wait_x, inv=invert, turn=turn, gu=gate_up, bk=back, rp=reduce_pair, act=activate, fwd=forward_grads, ex=expand_grads,
            dx=input_grad, fin=finish, hid=hidden, dy=take_dy,
        )
        for name, *where in plan:
            table[name](*where)
        for c in sends.values():
            c.wait_send()
        for c in recvs.values():
            c.wait_recv()
        for c in local.values():
            c.wait()

    plan0, plan1 = plans
    handed = tuple(m for m in range(2) if ("fin", m) in plan1)

    @pl.when(last)
    def _():
        run(True, plan1, ())

    @pl.when(sec == 0)
    def _():
        run(False, plan0, handed)


PLAN1 = (
    ("ax", 0), ("ady", 0), ("inv",), ("wx", 0), ("ax", 1), ("ady", 1), ("gu", 0), ("bk", 0), ("rp", 0, 0), ("rp", 0, 1),
    ("wx", 1), ("gu", 1), ("bk", 1), ("act", 0), ("rp", 1, 0), ("rp", 1, 1), ("fwd", 0), ("ex", 0), ("dx", 0), ("act", 1),
    ("fin", 0), ("fwd", 1), ("ex", 1), ("dx", 1), ("hid", 0), ("fin", 1), ("hid", 1),
)
PLAN0 = (
    ("ax", 0), ("ax", 1), ("inv",), ("wx", 0), ("gu", 0), ("wx", 1), ("gu", 1), ("rp", 0, 0), ("rp", 1, 0), ("turn",),
    ("dy", 0), ("bk", 0), ("rp", 0, 1), ("dy", 1), ("act", 0), ("bk", 1), ("fwd", 0), ("rp", 1, 1), ("ex", 0), ("dx", 0),
    ("act", 1), ("hid", 0), ("fwd", 1), ("ex", 1), ("dx", 1), ("hid", 1), ("fin", 0), ("fin", 1),
)


def relay_call(layer_input, top_grad, gate_weight, up_weight, down_weight, activity, plans=(PLAN0, PLAN1), number=1):
    any_space = pl.BlockSpec(memory_space=pl.ANY)
    hbm = pl.BlockSpec(memory_space=pltpu.HBM)
    dma = pltpu.SemaphoreType.DMA
    vm = pltpu.VMEM
    tile = (HALF, 16, 128)
    return pl.pallas_call(
        functools.partial(relay_kernel, plans),
        name="relay",
        out_shape=(
            jax.ShapeDtypeStruct((1, 2, 16, DL), BF16),
            jax.ShapeDtypeStruct((2, TOK, DL), BF16),
            jax.ShapeDtypeStruct((2, TOK, DL), BF16),
            jax.ShapeDtypeStruct((2, TOK, FL), BF16),
            jax.ShapeDtypeStruct((2, TOK, FL), BF16),
            jax.ShapeDtypeStruct((2, TOK, FL), BF16),
        ),
        in_specs=[hbm] * 6,
        out_specs=(any_space,) * 6,
        scratch_shapes=[
            vm((2, TOK, DL), BF16), vm((2, TOK, DL), BF16),
            vm((DL, FL), BF16), vm((DL, FL), BF16), vm((FL, DL), BF16),
            vm((FL, DL), BF16), vm((FL, DL), BF16), vm((DL, FL), BF16),
            vm((2, 3, 2, NBLK, 32, 128), F32),
            vm((2, 3, 4) + tile, F32), vm((2, 3, 4) + tile, F32),
            vm((2, 3) + tile, F32), vm((2, 3, 3) + tile, BF16), vm((2, 3, 3) + tile, BF16),
            vm((5, 2, 2) + tile, BF16), vm((5, 2, 2) + tile, BF16),
            vm((5, 2) + tile, BF16), vm((5, 2) + tile, BF16),
            vm((2, TOK, FL), BF16), vm((2, TOK, FL), BF16), vm((2, TOK, FL), BF16),
            vm((2, 2, TOK, DL // 2), F32), vm((2, 2, TOK, DL // 2), BF16), vm((2, 2, 7, 16, DL // 2), BF16),
            vm((2, 16, DL), BF16),
            pltpu.SMEM((1, 2, 2, 1, SLOTS), jnp.int32),
            pltpu.SMEM((2, 2, NBLK), jnp.int32), pltpu.SMEM((2, 2, NBLK), jnp.int32),
            dma((3,)), dma((5,)), dma((6, 2)),
            dma((2, 7)), dma((2, 7)), dma((2, 7)), dma((2, 7)),
            dma((2, 2)), dma((2, 2)), dma((2, 2, 3)), dma((2, 2, 3)),
            dma((2, 3)), dma((2, 3)), dma((2, 4)), dma((2, 4)),
            dma((2, 3)), dma((2, 3)), dma((2, 4)), dma((2, 4)),
            dma((2, 2, 7)), dma((2, 2, 7)), dma((2,)), dma((2,)),
        ],
        compiler_params=pltpu.CompilerParams(
            collective_id=number, has_side_effects=True, vmem_limit_bytes=48 * 2**20
        ),
        cost_estimate=pl.CostEstimate(flops=5 * 2**30, bytes_accessed=16 * 2**20, transcendentals=0),
    )(*(
        pltpu.with_memory_space_constraint(a, pltpu.HBM)
        for a in (layer_input, top_grad, gate_weight, up_weight, down_weight, activity)
    ))


def weights_kernel(x_ref, dy_ref, hid_ref, gh_ref, gu_ref, sent_ref, out_sent, og, ou, od, xt):
    @pl.when(pl.program_id(0) == 0)
    def _():
        xt[...] = x_ref[...].T
        out_sent[...] = sent_ref[...]

    og[0] = jnp.dot(xt[...], gh_ref[...], preferred_element_type=F32).astype(BF16)
    ou[0] = jnp.dot(xt[...], gu_ref[...], preferred_element_type=F32).astype(BF16)
    od[0] = lax.dot_general(hid_ref[...], dy_ref[...], TN, preferred_element_type=F32).astype(BF16)


def weights_call(x_all, dy_all, hid, gh, gu, sent):
    whole = lambda shape: pl.BlockSpec(shape, lambda j: (0,) * len(shape))
    cut = pl.BlockSpec((2 * TOK, 256), lambda j: (0, j))
    return pl.pallas_call(
        weights_kernel,
        name="weight_grads",
        grid=(FL // 256,),
        out_shape=(
            jax.ShapeDtypeStruct((1, 2, 16, DL), BF16),
            jax.ShapeDtypeStruct((1, DL, FL), BF16),
            jax.ShapeDtypeStruct((1, DL, FL), BF16),
            jax.ShapeDtypeStruct((1, FL, DL), BF16),
        ),
        in_specs=[whole((2 * TOK, DL)), whole((2 * TOK, DL)), cut, cut, cut, whole((1, 2, 16, DL))],
        out_specs=(
            whole((1, 2, 16, DL)),
            pl.BlockSpec((1, DL, 256), lambda j: (0, 0, j)),
            pl.BlockSpec((1, DL, 256), lambda j: (0, 0, j)),
            pl.BlockSpec((1, 256, DL), lambda j: (0, j, 0)),
        ),
        scratch_shapes=[pltpu.VMEM((DL, 2 * TOK), BF16)],
        compiler_params=pltpu.CompilerParams(
            dimension_semantics=("arbitrary",), vmem_limit_bytes=24 * 2**20
        ),
    )(x_all, dy_all, hid, gh, gu, sent)


def shards(layer_input, top_grad, gate_weight, up_weight, down_weight, activity):
    sent, x_all, dy_all, hid, gh, gu = relay_call(
        layer_input, top_grad, gate_weight, up_weight, down_weight, activity
    )
    flat = lambda a: a.reshape(2 * TOK, a.shape[-1])
    return weights_call(flat(x_all), flat(dy_all), flat(hid), flat(gh), flat(gu), sent)


def solution(mesh):
    in_specs = (
        P("section", None, "col", "row"),
        P(None, "col", "row"),
        P("section", "row", "col"),
        P("section", "row", "col"),
        P("section", "col", "row"),
        P("section", None, None, "col", None),
    )
    out_specs = (
        P("section", None, "col", "row"),
        P("section", "row", "col"),
        P("section", "row", "col"),
        P("section", "col", "row"),
    )
    return jax.shard_map(shards, mesh=mesh, in_specs=in_specs, out_specs=out_specs, check_vma=False)
```

```python
import functools

import jax
import jax.numpy as jnp
from jax import lax
from jax.experimental import pallas as pl
from jax.experimental.pallas import tpu as pltpu
from jax.sharding import PartitionSpec as P

MESH = pl.DeviceIdType.MESH
F32, BF16 = jnp.float32, jnp.bfloat16
NT = (((1,), (1,)), ((), ()))
TN = (((0,), (0,)), ((), ()))

BLK = 64
TOK = 128
DL = 1024
FL = 1792
NBLK = 28
SLOTS = 14
HALF = 7
COL_STEPS = ((1, 0), (3, 0), (2, 0), (0, 1), (1, 1), (3, 1), (2, 1))


def relay_kernel(
    plans,
    x_hbm, top_hbm, wg_hbm, wu_hbm, wd_hbm, act_hbm,
    sent_hbm, xt_hbm, dyall_hbm, hid_hbm, gh_hbm, gu_hbm,
    xs, xt, dys, wg, wu, wd, wgt, wut, wdt, dn, ps, pr, yo, ys, yr,
    agb0, agb1, agh0, agh1, hid, gh, gu, dxf, dxs, rr, sentv, act_ref, inv_y, inv_i,
    w_sem, own_sem, out_sem,
    x_s, x_r, dy_s, dy_r, pair_s, pair_r, y_s, y_r,
    ag_s, ag_r, agp_s, agp_r, hg_s, hg_r, hgp_s, hgp_r, rs_s, rs_r, hand_s, hand_r,
):
    agb, agh = (agb0, agb1), (agh0, agh1)
    sec, row, col = (lax.axis_index(a) for a in ("section", "row", "col"))
    y, k = row // 2, lax.rem(row, 2)
    z, xl = col // 2, lax.rem(col, 2)
    last = sec == 1

    def at_col(step, sign=1):
        dz, dx = step
        zz = lax.rem(z + (dz if sign > 0 else 4 - dz), 4)
        return zz * 2 + ((1 - xl) if dx else xl)

    def col_dev(step, sign=1):
        return (sec, row, at_col(step, sign))

    def y_at(d):
        return lax.rem(y + d, 4)

    def y_dev(d):
        return (sec, y_at(d) * 2 + k, col)

    pair = (sec, 2 * y + 1 - k, col)
    relay = (1 - sec, row, 2 * z + 1 - xl)

    def remote(src, dst, ss, rs, dev):
        return pltpu.make_async_remote_copy(
            src_ref=src, dst_ref=dst, send_sem=ss, recv_sem=rs, device_id=dev, device_id_type=MESH
        )

    def rows16(c):
        return pl.ds(pl.multiple_of(c * 16, 16), 16)

    lists = pltpu.make_async_copy(act_hbm, act_ref, own_sem.at[4])
    weights = [
        pltpu.make_async_copy(src.at[0], dst, w_sem.at[i])
        for i, (src, dst) in enumerate(((wg_hbm, wg), (wu_hbm, wu), (wd_hbm, wd)))
    ]
    own_x = [
        pltpu.make_async_copy(x_hbm.at[0, m], xs.at[m, rows16(col)], own_sem.at[m]) for m in range(2)
    ]
    own_dy = [
        pltpu.make_async_copy(top_hbm.at[m], dys.at[m, rows16(col)], own_sem.at[2 + m])
        for m in range(2)
    ]
    lists.start()
    for c in own_x:
        c.start()
    for c in weights:
        c.start()

    barrier = pltpu.get_barrier_semaphore()
    partners = [col_dev(s) for s in COL_STEPS] + [y_dev(d) for d in (1, 2, 3)] + [pair, relay]
    for dev in partners:
        pl.semaphore_signal(barrier, inc=1, device_id=dev, device_id_type=MESH)
    pl.semaphore_wait(barrier, len(partners))

    def invert():
        lists.wait()
        for m in range(2):
            agb[m][4] = jnp.zeros(agb[m].shape[1:], BF16)
            agh[m][4] = jnp.zeros(agh[m].shape[1:], BF16)
            for tb in range(2):
                def body(n, _):
                    slot = jnp.int32(2 * SLOTS)
                    for s in range(SLOTS):
                        slot = jnp.where(act_ref[0, m, tb, 0, s] == n, s, slot)
                    inv_y[m, tb, n] = jnp.where(slot < SLOTS, 2 * tb + jnp.where(slot < HALF, 0, 1), 4)
                    inv_i[m, tb, n] = jnp.where(
                        slot < SLOTS, jnp.where(slot < HALF, slot, slot - HALF), 0
                    )
                    return 0

                lax.fori_loop(0, NBLK, body, 0)

    left = lax.broadcasted_iota(jnp.int32, (32, 128), 1) < 64
    left16 = lax.broadcasted_iota(jnp.int32, (16, 128), 1) < 64
    MATS = ((0, 2), (2, 1))
    far_first = (6, 4, 5, 2, 3, 0, 1)
    halves = (pl.ds(0, DL // 2), pl.ds(DL // 2, DL // 2))

    def run(is_last, plan, expected):
        sends, recvs, local = {}, {}, {}

        def start(key, src, dst, ss, rs, dev, landing=None):
            c = remote(src, dst, ss, rs, dev)
            c.start()
            sends[key] = c
            if landing is not None:
                recvs[key] = remote(landing, landing, ss, rs, dev)

        def arrived(*key):
            recvs.pop(key).wait_recv()

        local.update({("w", i): c for i, c in enumerate(weights)})
        local.update({("x", m): c for m, c in enumerate(own_x)})

        def start_local(key, src, dst, sem):
            c = pltpu.make_async_copy(src, dst, sem)
            c.start()
            local[key] = c

        def dy_block(c):
            return c if is_last else c + 1 - 2 * lax.rem(c, 2)

        def lay_out(acc, m, mat, j):
            for tb in range(2):
                for h in range(2):
                    lo = acc[64 * tb : 64 * tb + 32, 128 * h : 128 * h + 128]
                    hi = acc[64 * tb + 32 : 64 * tb + 64, 128 * h : 128 * h + 128]
                    dn[m, mat, tb, 4 * j + 2 * h] = jnp.where(left, lo, pltpu.roll(hi, 64, 1))
                    dn[m, mat, tb, 4 * j + 2 * h + 1] = jnp.where(left, pltpu.roll(lo, 64, 1), hi)

        def send_pair(m, j):
            lo, n = MATS[j]
            far = pl.ds(pl.multiple_of(16 * (1 - k), 16), 16)

            def body(i, _):
                for yy in range(4):
                    tb, sh = yy // 2, yy % 2
                    b = jnp.minimum(act_ref[0, m, tb, 0, sh * HALF + i], NBLK - 1)
                    for mat in range(lo, lo + n):
                        ps[m, mat, yy, i] = dn[m, mat, tb, b, far, :]
                return 0

            lax.fori_loop(0, HALF, body, 0, unroll=True)
            cut = pl.ds(lo, n)
            start(
                ("pair", m, j), ps.at[m, cut], pr.at[m, cut], pair_s.at[m, j], pair_r.at[m, j], pair,
                pr.at[m, cut],
            )

        def spread_x(m):
            for i in far_first:
                step = COL_STEPS[i]
                start(
                    ("x", m, i), x_hbm.at[0, m], xs.at[m, rows16(col)], x_s.at[m, i], x_r.at[m, i],
                    col_dev(step), xs.at[m, rows16(at_col(step, -1))],
                )

        def spread_top(m):
            own_dy[m].start()
            local["dy", m] = own_dy[m]
            for half in range(2):
                spread_dy(m, half, top_hbm.at[m, :, halves[half]])

        def wait_x(m):
            local.pop(("x", m)).wait()
            for i in range(7):
                arrived("x", m, i)

        def spread_dy(m, half, src):
            block = rows16(dy_block(col))
            cols = halves[half]
            for i in far_first:
                step = COL_STEPS[i]
                start(
                    ("dy", m, half, i), src, dys.at[m, block, cols], dy_s.at[m, half, i], dy_r.at[m, half, i],
                    col_dev(step), dys.at[m, rows16(dy_block(at_col(step, -1))), cols],
                )

        def take_dy(m):
            for half in range(2):
                arrived("hand", m, half)
                spread_dy(m, half, dys.at[m, rows16(dy_block(col)), halves[half]])

        def gate_up(m):
            def body(j, _):
                cut = pl.ds(pl.multiple_of(j * 256, 256), 256)
                lay_out(jnp.dot(xs[m], wg[:, cut], preferred_element_type=F32), m, 0, j)
                lay_out(jnp.dot(xs[m], wu[:, cut], preferred_element_type=F32), m, 1, j)
                return 0

            lax.fori_loop(0, 7, body, 0, unroll=True)
            send_pair(m, 0)

        def back(m):
            if is_last:
                local.pop(("dy", m)).wait()
            for half in range(2):
                for i in range(7):
                    arrived("dy", m, half, i)
            start_local((1, m), dys.at[m], dyall_hbm.at[m], out_sem.at[1, m])

            def body(j, _):
                cut = pl.ds(pl.multiple_of(j * 256, 256), 256)
                grad = jnp.dot(dys[m], wdt[:, cut], preferred_element_type=F32)
                lay_out(grad, m, 2, j)
                return 0

            lax.fori_loop(0, 7, body, 0, unroll=True)
            send_pair(m, 1)

        def reduce_pair(m, j):
            arrived("pair", m, j)
            lo, n = MATS[j]
            near = pl.ds(pl.multiple_of(16 * k, 16), 16)
            cut = pl.ds(lo, n)
            for d in (2, 1, 3, 0):
                yy = y_at(d)
                tb, sh = yy // 2, lax.rem(yy, 2)

                def body(i, _):
                    b = jnp.minimum(act_ref[0, m, tb, 0, sh * HALF + i], NBLK - 1)
                    for mat in range(lo, lo + n):
                        total = dn[m, mat, tb, b, near, :] + pr[m, mat, yy, i]
                        if d:
                            ys[m, d - 1, mat, i] = total.astype(BF16)
                        else:
                            yo[m, mat, i] = total
                    return 0

                lax.fori_loop(0, HALF, body, 0, unroll=True)
                if d:
                    start(
                        ("y", m, j, d), ys.at[m, d - 1, cut], yr.at[m, d - 1, cut],
                        y_s.at[m, j, d - 1], y_r.at[m, j, d - 1], y_dev(d), yr.at[m, d - 1, cut],
                    )

        def spread(name, buf, m, sems):
            ss, rs, pss, prs = sems
            for d in (2, 1, 3):
                start(
                    (name, m, d), buf.at[y, k], buf.at[y, k], ss.at[m, d - 1], rs.at[m, d - 1], y_dev(d),
                    buf.at[y_at(4 - d), k],
                )
            start((name + "p", m, 0), buf.at[y, k], buf.at[y, k], pss.at[m, 0], prs.at[m, 0], pair, buf.at[y, 1 - k])

        def forward(name, buf, m, sems):
            ss, rs, pss, prs = sems
            for d in (1, 3, 2):
                arrived(name, m, d)
                yy = y_at(4 - d)
                start(
                    (name + "p", m, d), buf.at[yy, k], buf.at[yy, k], pss.at[m, d], prs.at[m, d], pair,
                    buf.at[yy, 1 - k],
                )

        grad_sems, hid_sems = (ag_s, ag_r, agp_s, agp_r), (hg_s, hg_r, hgp_s, hgp_r)

        def total(m, mat, i):
            value = yo[m, mat, i]
            for d in range(3):
                value = value + yr[m, d, mat, i].astype(F32)
            return value

        def gate_sums(m):
            for d in (1, 2, 3):
                arrived("y", m, 0, d)

            def body(i, _):
                r = jnp.maximum(total(m, 0, i), 0.0)
                up = total(m, 1, i)
                yo[m, 0, i] = r
                yo[m, 1, i] = up
                agh[m][y, k, i] = (r * r * up).astype(BF16)
                return 0

            lax.fori_loop(0, HALF, body, 0, unroll=True)

        def activate(m):
            for d in (1, 2, 3):
                arrived("y", m, 1, d)

            def body(i, _):
                r, up, grad = yo[m, 0, i], yo[m, 1, i], total(m, 2, i)
                agb[m][y, k, 0, i] = (2.0 * r * up * grad).astype(BF16)
                agb[m][y, k, 1, i] = (r * r * grad).astype(BF16)
                return 0

            lax.fori_loop(0, HALF, body, 0, unroll=True)
            spread("g", agb[m], m, grad_sems)

        def spread_hidden(m):
            spread("h", agh[m], m, hid_sems)

        def forward_grads(m):
            forward("g", agb[m], m, grad_sems)

        def expand(m, sources, targets):
            def body(n, _):
                cut = pl.ds(pl.multiple_of(n * 128, 128), 128)
                for tb in range(2):
                    ya, ia = inv_y[m, tb, 2 * n], inv_i[m, tb, 2 * n]
                    yb, ib = inv_y[m, tb, 2 * n + 1], inv_i[m, tb, 2 * n + 1]
                    for kk in range(2):
                        for src, dst in zip(sources, targets):
                            a = src(ya, kk, ia).astype(F32)
                            b = src(yb, kk, ib).astype(F32)
                            top = 64 * tb + 16 * kk
                            dst[m, top : top + 16, cut] = jnp.where(left16, a, pltpu.roll(b, 64, 1)).astype(BF16)
                            dst[m, top + 32 : top + 48, cut] = jnp.where(left16, pltpu.roll(a, 64, 1), b).astype(BF16)
                return 0

            lax.fori_loop(0, NBLK // 2, body, 0, unroll=True)

        def expand_grads(m):
            for d in (0, 1, 3, 2):
                arrived("gp", m, d)
            expand(
                m, (lambda a, b, c: agb[m][a, b, 0, c], lambda a, b, c: agb[m][a, b, 1, c]), (gh, gu)
            )
            start_local((3, m), gh.at[m], gh_hbm.at[m], out_sem.at[3, m])
            start_local((4, m), gu.at[m], gu_hbm.at[m], out_sem.at[4, m])

        def input_grad(m):
            def body(j, half):
                cut = pl.ds(pl.multiple_of(j * 256, 256), 256)
                rows = pl.ds(pl.multiple_of(half * 512 + j * 256, 256), 256)
                part = jnp.dot(gh[m], wgt[:, rows], preferred_element_type=F32)
                part = part + jnp.dot(gu[m], wut[:, rows], preferred_element_type=F32)
                dxf[m, half, :, cut] = part
                dxs[m, half, :, cut] = part.astype(BF16)

            for half in range(2):
                lax.fori_loop(0, 2, lambda j, c: (body(j, half), c)[1], 0, unroll=True)
                for i in far_first:
                    start(
                        ("rs", m, half, i), dxs.at[m, half, rows16(at_col(COL_STEPS[i]))], rr.at[m, half, i],
                        rs_s.at[m, half, i], rs_r.at[m, half, i], col_dev(COL_STEPS[i]), rr.at[m, half, i],
                    )

        def finish(m):
            for half in range(2):
                cols = slice(512 * half, 512 * half + 512)
                for i in range(7):
                    arrived("rs", m, half, i)
                total = dys[m, rows16(col), cols].astype(F32) + dxf[m, half, rows16(col), :]
                for i in range(7):
                    total = total + rr[m, half, i].astype(F32)
                sentv[m, :, cols] = total.astype(BF16)
                if is_last:
                    start(
                        ("hand", m, half), sentv.at[m, :, halves[half]], dys.at[m, rows16(col), halves[half]],
                        hand_s.at[m, half], hand_r.at[m, half], relay,
                    )
            start_local((5, m), sentv.at[m], sent_hbm.at[0, m], out_sem.at[5, m])

        def turn():
            for i, (src, dst) in enumerate(((wg, wgt), (wu, wut))):
                local.pop(("w", i)).wait()

                def body(j, _):
                    cut = pl.ds(pl.multiple_of(j * 256, 256), 256)
                    dst[cut, :] = src[:, cut].T
                    return 0

                lax.fori_loop(0, 7, body, 0)
            local.pop(("w", 2)).wait()

            def body(j, _):
                cut = pl.ds(pl.multiple_of(j * 256, 256), 256)
                wdt[:, cut] = wd[cut, :].T
                return 0

            lax.fori_loop(0, 7, body, 0)

        def turn_x():
            for m in range(2):
                xt[:, TOK * m : TOK * m + TOK] = xs[m].T
            start_local((0, 0), xt, xt_hbm, out_sem.at[0, 0])

        def hidden(m):
            forward("h", agh[m], m, hid_sems)
            for d in range(4):
                arrived("hp", m, d)
            expand(m, (lambda a, b, c: agh[m][a, b, c],), (hid,))
            start_local((2, m), hid.at[m], hid_hbm.at[m], out_sem.at[2, m])

        for m in expected:
            for half in range(2):
                block = dys.at[m, rows16(dy_block(col)), halves[half]]
                recvs["hand", m, half] = remote(block, block, hand_s.at[m, half], hand_r.at[m, half], relay)
        table = dict(
            ax=spread_x, ady=spread_top, wx=wait_x, inv=invert, turn=turn, gu=gate_up, gs=gate_sums, hs=spread_hidden, xt=turn_x, bk=back, rp=reduce_pair, act=activate, fwd=forward_grads, ex=expand_grads,
            dx=input_grad, fin=finish, hid=hidden, dy=take_dy,
        )
        for name, *where in plan:
            table[name](*where)
        for c in sends.values():
            c.wait_send()
        for c in recvs.values():
            c.wait_recv()
        for c in local.values():
            c.wait()

    plan0, plan1 = plans
    handed = tuple(m for m in range(2) if ("fin", m) in plan1)

    @pl.when(last)
    def _():
        run(True, plan1, ())

    @pl.when(sec == 0)
    def _():
        run(False, plan0, handed)


PLAN1 = (
    ("ax", 0), ("inv",), ("ady", 0), ("turn",), ("wx", 0), ("ax", 1), ("ady", 1), ("gu", 0), ("bk", 0), ("rp", 0, 0),
    ("rp", 0, 1), ("wx", 1), ("gu", 1), ("gs", 0), ("rp", 1, 0), ("bk", 1), ("act", 0), ("rp", 1, 1), ("fwd", 0),
    ("ex", 0), ("gs", 1), ("act", 1), ("dx", 0), ("fwd", 1), ("ex", 1), ("fin", 0), ("dx", 1), ("fin", 1),
    ("hs", 0), ("hs", 1), ("xt",), ("hid", 0), ("hid", 1),
)
PLAN0 = (
    ("ax", 0), ("ax", 1), ("inv",), ("turn",), ("wx", 0), ("gu", 0), ("wx", 1), ("gu", 1), ("rp", 0, 0), ("rp", 1, 0),
    ("gs", 0), ("hs", 0), ("gs", 1), ("hs", 1), ("xt",), ("hid", 0), ("hid", 1), ("dy", 0), ("bk", 0), ("rp", 0, 1),
    ("dy", 1), ("act", 0), ("bk", 1), ("rp", 1, 1), ("fwd", 0), ("ex", 0), ("act", 1), ("dx", 0), ("fwd", 1),
    ("ex", 1), ("fin", 0), ("dx", 1), ("fin", 1),
)


def relay_call(layer_input, top_grad, gate_weight, up_weight, down_weight, activity, plans=(PLAN0, PLAN1), number=1):
    any_space = pl.BlockSpec(memory_space=pl.ANY)
    hbm = pl.BlockSpec(memory_space=pltpu.HBM)
    dma = pltpu.SemaphoreType.DMA
    vm = pltpu.VMEM
    tile = (HALF, 16, 128)
    return pl.pallas_call(
        functools.partial(relay_kernel, plans),
        name="relay",
        out_shape=(
            jax.ShapeDtypeStruct((1, 2, 16, DL), BF16),
            jax.ShapeDtypeStruct((DL, 2 * TOK), BF16),
            jax.ShapeDtypeStruct((2, TOK, DL), BF16),
            jax.ShapeDtypeStruct((2, TOK, FL), BF16),
            jax.ShapeDtypeStruct((2, TOK, FL), BF16),
            jax.ShapeDtypeStruct((2, TOK, FL), BF16),
        ),
        in_specs=[hbm] * 6,
        out_specs=(any_space,) * 6,
        scratch_shapes=[
            vm((2, TOK, DL), BF16), vm((DL, 2 * TOK), BF16), vm((2, TOK, DL), BF16),
            vm((DL, FL), BF16), vm((DL, FL), BF16), vm((FL, DL), BF16),
            vm((FL, DL), BF16), vm((FL, DL), BF16), vm((DL, FL), BF16),
            vm((2, 3, 2, NBLK, 32, 128), F32),
            vm((2, 3, 4) + tile, F32), vm((2, 3, 4) + tile, F32),
            vm((2, 3) + tile, F32), vm((2, 3, 3) + tile, BF16), vm((2, 3, 3) + tile, BF16),
            vm((5, 2, 2) + tile, BF16), vm((5, 2, 2) + tile, BF16),
            vm((5, 2) + tile, BF16), vm((5, 2) + tile, BF16),
            vm((2, TOK, FL), BF16), vm((2, TOK, FL), BF16), vm((2, TOK, FL), BF16),
            vm((2, 2, TOK, DL // 2), F32), vm((2, 2, TOK, DL // 2), BF16), vm((2, 2, 7, 16, DL // 2), BF16),
            vm((2, 16, DL), BF16),
            pltpu.SMEM((1, 2, 2, 1, SLOTS), jnp.int32),
            pltpu.SMEM((2, 2, NBLK), jnp.int32), pltpu.SMEM((2, 2, NBLK), jnp.int32),
            dma((3,)), dma((5,)), dma((6, 2)),
            dma((2, 7)), dma((2, 7)), dma((2, 2, 7)), dma((2, 2, 7)),
            dma((2, 2)), dma((2, 2)), dma((2, 2, 3)), dma((2, 2, 3)),
            dma((2, 3)), dma((2, 3)), dma((2, 4)), dma((2, 4)),
            dma((2, 3)), dma((2, 3)), dma((2, 4)), dma((2, 4)),
            dma((2, 2, 7)), dma((2, 2, 7)), dma((2, 2)), dma((2, 2)),
        ],
        compiler_params=pltpu.CompilerParams(
            collective_id=number, has_side_effects=True, vmem_limit_bytes=48 * 2**20
        ),
        cost_estimate=pl.CostEstimate(flops=5 * 2**30, bytes_accessed=16 * 2**20, transcendentals=0),
    )(*(
        pltpu.with_memory_space_constraint(a, pltpu.HBM)
        for a in (layer_input, top_grad, gate_weight, up_weight, down_weight, activity)
    ))


def weights_kernel(xt_ref, dy_ref, hid_ref, gh_ref, gu_ref, sent_ref, out_sent, og, ou, od):
    @pl.when(pl.program_id(0) == 0)
    def _():
        out_sent[...] = sent_ref[...]

    cut = pl.ds(pl.multiple_of(pl.program_id(0) * 256, 256), 256)
    og[0] = jnp.dot(xt_ref[...], gh_ref[:, cut], preferred_element_type=F32).astype(BF16)
    ou[0] = jnp.dot(xt_ref[...], gu_ref[:, cut], preferred_element_type=F32).astype(BF16)
    od[0] = lax.dot_general(hid_ref[:, cut], dy_ref[...], TN, preferred_element_type=F32).astype(BF16)


def weights_call(xt, dy_all, hid, gh, gu, sent):
    whole = lambda shape: pl.BlockSpec(shape, lambda j: (0,) * len(shape))
    return pl.pallas_call(
        weights_kernel,
        name="weight_grads",
        grid=(FL // 256,),
        out_shape=(
            jax.ShapeDtypeStruct((1, 2, 16, DL), BF16),
            jax.ShapeDtypeStruct((1, DL, FL), BF16),
            jax.ShapeDtypeStruct((1, DL, FL), BF16),
            jax.ShapeDtypeStruct((1, FL, DL), BF16),
        ),
        in_specs=[pl.BlockSpec(memory_space=pltpu.VMEM)] * 6,
        out_specs=(
            whole((1, 2, 16, DL)),
            pl.BlockSpec((1, DL, 256), lambda j: (0, 0, j)),
            pl.BlockSpec((1, DL, 256), lambda j: (0, 0, j)),
            pl.BlockSpec((1, 256, DL), lambda j: (0, j, 0)),
        ),
        compiler_params=pltpu.CompilerParams(
            dimension_semantics=("arbitrary",), vmem_limit_bytes=24 * 2**20
        ),
    )(xt, dy_all, hid, gh, gu, sent)


def shards(layer_input, top_grad, gate_weight, up_weight, down_weight, activity):
    sent, xt, dy_all, hid, gh, gu = relay_call(
        layer_input, top_grad, gate_weight, up_weight, down_weight, activity
    )
    flat = lambda a: a.reshape(2 * TOK, a.shape[-1])
    return weights_call(xt, flat(dy_all), flat(hid), flat(gh), flat(gu), sent)


def solution(mesh):
    in_specs = (
        P("section", None, "col", "row"),
        P(None, "col", "row"),
        P("section", "row", "col"),
        P("section", "row", "col"),
        P("section", "col", "row"),
        P("section", None, None, "col", None),
    )
    out_specs = (
        P("section", None, "col", "row"),
        P("section", "row", "col"),
        P("section", "row", "col"),
        P("section", "col", "row"),
    )
    return jax.shard_map(shards, mesh=mesh, in_specs=in_specs, out_specs=out_specs, check_vma=False)
```

```python
import functools

import jax
import jax.numpy as jnp
from jax import lax
from jax.experimental import pallas as pl
from jax.experimental.pallas import tpu as pltpu
from jax.sharding import PartitionSpec as P

MESH = pl.DeviceIdType.MESH
F32, BF16 = jnp.float32, jnp.bfloat16
NT = (((1,), (1,)), ((), ()))
TN = (((0,), (0,)), ((), ()))

BLK = 64
TOK = 128
DL = 1024
FL = 1792
NBLK = 28
SLOTS = 14
HALF = 7
COL_STEPS = ((1, 0), (3, 0), (2, 0), (0, 1), (1, 1), (3, 1), (2, 1))


def relay_kernel(
    plans,
    x_hbm, top_hbm, wg_hbm, wu_hbm, wd_hbm, act_hbm,
    sent_ref, xt_hbm, dyall_hbm, hid_hbm, gh_hbm, gu_hbm,
    xs, xt, dys, wg, wu, wd, wgt, wut, wdt, dn, ps, pr, yo, ys, yr,
    agb0, agb1, agh0, agh1, hid, gh, gu, dxf, dxs, rr, act_ref, inv_y, inv_i,
    w_sem, own_sem, out_sem,
    x_s, x_r, dy_s, dy_r, pair_s, pair_r, y_s, y_r,
    ag_s, ag_r, agp_s, agp_r, hg_s, hg_r, hgp_s, hgp_r, rs_s, rs_r, hand_s, hand_r,
):
    agb, agh = (agb0, agb1), (agh0, agh1)
    sec, row, col = (lax.axis_index(a) for a in ("section", "row", "col"))
    y, k = row // 2, lax.rem(row, 2)
    z, xl = col // 2, lax.rem(col, 2)
    last = sec == 1

    def at_col(step, sign=1):
        dz, dx = step
        zz = lax.rem(z + (dz if sign > 0 else 4 - dz), 4)
        return zz * 2 + ((1 - xl) if dx else xl)

    def col_dev(step, sign=1):
        return (sec, row, at_col(step, sign))

    def y_at(d):
        return lax.rem(y + d, 4)

    def y_dev(d):
        return (sec, y_at(d) * 2 + k, col)

    pair = (sec, 2 * y + 1 - k, col)
    relay = (1 - sec, row, 2 * z + 1 - xl)

    def remote(src, dst, ss, rs, dev):
        return pltpu.make_async_remote_copy(
            src_ref=src, dst_ref=dst, send_sem=ss, recv_sem=rs, device_id=dev, device_id_type=MESH
        )

    def rows16(c):
        return pl.ds(pl.multiple_of(c * 16, 16), 16)

    lists = pltpu.make_async_copy(act_hbm, act_ref, own_sem.at[4])
    weights = [
        pltpu.make_async_copy(src.at[0], dst, w_sem.at[i])
        for i, (src, dst) in enumerate(((wg_hbm, wg), (wu_hbm, wu), (wd_hbm, wd)))
    ]
    own_x = [
        pltpu.make_async_copy(x_hbm.at[0, m], xs.at[m, rows16(col)], own_sem.at[m]) for m in range(2)
    ]
    own_dy = [
        pltpu.make_async_copy(top_hbm.at[m], dys.at[m, rows16(col)], own_sem.at[2 + m])
        for m in range(2)
    ]
    lists.start()
    for c in own_x:
        c.start()
    for c in weights:
        c.start()

    barrier = pltpu.get_barrier_semaphore()
    partners = [col_dev(s) for s in COL_STEPS] + [y_dev(d) for d in (1, 2, 3)] + [pair, relay]
    for dev in partners:
        pl.semaphore_signal(barrier, inc=1, device_id=dev, device_id_type=MESH)
    pl.semaphore_wait(barrier, len(partners))

    def invert():
        lists.wait()
        for m in range(2):
            agb[m][4] = jnp.zeros(agb[m].shape[1:], BF16)
            agh[m][4] = jnp.zeros(agh[m].shape[1:], BF16)
            for tb in range(2):
                def body(n, _):
                    slot = jnp.int32(2 * SLOTS)
                    for s in range(SLOTS):
                        slot = jnp.where(act_ref[0, m, tb, 0, s] == n, s, slot)
                    inv_y[m, tb, n] = jnp.where(slot < SLOTS, 2 * tb + jnp.where(slot < HALF, 0, 1), 4)
                    inv_i[m, tb, n] = jnp.where(
                        slot < SLOTS, jnp.where(slot < HALF, slot, slot - HALF), 0
                    )
                    return 0

                lax.fori_loop(0, NBLK, body, 0)

    left = lax.broadcasted_iota(jnp.int32, (32, 128), 1) < 64
    left16 = lax.broadcasted_iota(jnp.int32, (16, 128), 1) < 64
    MATS = ((0, 2), (2, 1))
    far_first = (6, 4, 5, 2, 3, 0, 1)
    halves = (pl.ds(0, DL // 2), pl.ds(DL // 2, DL // 2))

    def run(is_last, plan, expected):
        sends, recvs, local = {}, {}, {}

        def start(key, src, dst, ss, rs, dev, landing=None):
            c = remote(src, dst, ss, rs, dev)
            c.start()
            sends[key] = c
            if landing is not None:
                recvs[key] = remote(landing, landing, ss, rs, dev)

        def arrived(*key):
            recvs.pop(key).wait_recv()

        local.update({("w", i): c for i, c in enumerate(weights)})
        local.update({("x", m): c for m, c in enumerate(own_x)})

        def start_local(key, src, dst, sem):
            c = pltpu.make_async_copy(src, dst, sem)
            c.start()
            local[key] = c

        def dy_block(c):
            return c if is_last else c + 1 - 2 * lax.rem(c, 2)

        def lay_out(acc, m, mat, j):
            for tb in range(2):
                for h in range(2):
                    lo = acc[64 * tb : 64 * tb + 32, 128 * h : 128 * h + 128]
                    hi = acc[64 * tb + 32 : 64 * tb + 64, 128 * h : 128 * h + 128]
                    dn[m, mat, tb, 4 * j + 2 * h] = jnp.where(left, lo, pltpu.roll(hi, 64, 1))
                    dn[m, mat, tb, 4 * j + 2 * h + 1] = jnp.where(left, pltpu.roll(lo, 64, 1), hi)

        def send_pair(m, j):
            lo, n = MATS[j]
            far = pl.ds(pl.multiple_of(16 * (1 - k), 16), 16)

            def body(i, _):
                for yy in range(4):
                    tb, sh = yy // 2, yy % 2
                    b = jnp.minimum(act_ref[0, m, tb, 0, sh * HALF + i], NBLK - 1)
                    for mat in range(lo, lo + n):
                        ps[m, mat, yy, i] = dn[m, mat, tb, b, far, :]
                return 0

            lax.fori_loop(0, HALF, body, 0, unroll=True)
            cut = pl.ds(lo, n)
            start(
                ("pair", m, j), ps.at[m, cut], pr.at[m, cut], pair_s.at[m, j], pair_r.at[m, j], pair,
                pr.at[m, cut],
            )

        def spread_x(m):
            for i in far_first:
                step = COL_STEPS[i]
                start(
                    ("x", m, i), x_hbm.at[0, m], xs.at[m, rows16(col)], x_s.at[m, i], x_r.at[m, i],
                    col_dev(step), xs.at[m, rows16(at_col(step, -1))],
                )

        def spread_top(m):
            own_dy[m].start()
            local["dy", m] = own_dy[m]
            for half in range(2):
                spread_dy(m, half, top_hbm.at[m, :, halves[half]])

        def wait_x(m):
            local.pop(("x", m)).wait()
            for i in range(7):
                arrived("x", m, i)

        def spread_dy(m, half, src):
            block = rows16(dy_block(col))
            cols = halves[half]
            for i in far_first:
                step = COL_STEPS[i]
                start(
                    ("dy", m, half, i), src, dys.at[m, block, cols], dy_s.at[m, half, i], dy_r.at[m, half, i],
                    col_dev(step), dys.at[m, rows16(dy_block(at_col(step, -1))), cols],
                )

        def take_dy(m):
            for half in range(2):
                arrived("hand", m, half)
                spread_dy(m, half, dys.at[m, rows16(dy_block(col)), halves[half]])

        def gate_up(m):
            def body(j, _):
                cut = pl.ds(pl.multiple_of(j * 256, 256), 256)
                lay_out(jnp.dot(xs[m], wg[:, cut], preferred_element_type=F32), m, 0, j)
                lay_out(jnp.dot(xs[m], wu[:, cut], preferred_element_type=F32), m, 1, j)
                return 0

            lax.fori_loop(0, 7, body, 0, unroll=True)
            send_pair(m, 0)

        def back(m):
            if is_last:
                local.pop(("dy", m)).wait()
            for half in range(2):
                for i in range(7):
                    arrived("dy", m, half, i)
            start_local((1, m), dys.at[m], dyall_hbm.at[m], out_sem.at[1, m])

            def body(j, _):
                cut = pl.ds(pl.multiple_of(j * 256, 256), 256)
                grad = jnp.dot(dys[m], wdt[:, cut], preferred_element_type=F32)
                lay_out(grad, m, 2, j)
                return 0

            lax.fori_loop(0, 7, body, 0, unroll=True)
            send_pair(m, 1)

        def reduce_pair(m, j):
            arrived("pair", m, j)
            lo, n = MATS[j]
            near = pl.ds(pl.multiple_of(16 * k, 16), 16)
            cut = pl.ds(lo, n)
            for d in (2, 1, 3, 0):
                yy = y_at(d)
                tb, sh = yy // 2, lax.rem(yy, 2)

                def body(i, _):
                    b = jnp.minimum(act_ref[0, m, tb, 0, sh * HALF + i], NBLK - 1)
                    for mat in range(lo, lo + n):
                        total = dn[m, mat, tb, b, near, :] + pr[m, mat, yy, i]
                        if d:
                            ys[m, d - 1, mat, i] = total.astype(BF16)
                        else:
                            yo[m, mat, i] = total
                    return 0

                lax.fori_loop(0, HALF, body, 0, unroll=True)
                if d:
                    start(
                        ("y", m, j, d), ys.at[m, d - 1, cut], yr.at[m, d - 1, cut],
                        y_s.at[m, j, d - 1], y_r.at[m, j, d - 1], y_dev(d), yr.at[m, d - 1, cut],
                    )

        def spread(name, buf, m, sems):
            ss, rs, pss, prs = sems
            for d in (2, 1, 3):
                start(
                    (name, m, d), buf.at[y, k], buf.at[y, k], ss.at[m, d - 1], rs.at[m, d - 1], y_dev(d),
                    buf.at[y_at(4 - d), k],
                )
            start((name + "p", m, 0), buf.at[y, k], buf.at[y, k], pss.at[m, 0], prs.at[m, 0], pair, buf.at[y, 1 - k])

        def forward(name, buf, m, sems):
            ss, rs, pss, prs = sems
            for d in (1, 3, 2):
                arrived(name, m, d)
                yy = y_at(4 - d)
                start(
                    (name + "p", m, d), buf.at[yy, k], buf.at[yy, k], pss.at[m, d], prs.at[m, d], pair,
                    buf.at[yy, 1 - k],
                )

        grad_sems, hid_sems = (ag_s, ag_r, agp_s, agp_r), (hg_s, hg_r, hgp_s, hgp_r)

        def total(m, mat, i):
            value = yo[m, mat, i]
            for d in range(3):
                value = value + yr[m, d, mat, i].astype(F32)
            return value

        def gate_sums(m):
            for d in (1, 2, 3):
                arrived("y", m, 0, d)

            def body(i, _):
                r = jnp.maximum(total(m, 0, i), 0.0)
                up = total(m, 1, i)
                yo[m, 0, i] = r
                yo[m, 1, i] = up
                agh[m][y, k, i] = (r * r * up).astype(BF16)
                return 0

            lax.fori_loop(0, HALF, body, 0, unroll=True)

        def activate(m):
            for d in (1, 2, 3):
                arrived("y", m, 1, d)

            def body(i, _):
                r, up, grad = yo[m, 0, i], yo[m, 1, i], total(m, 2, i)
                agb[m][y, k, 0, i] = (2.0 * r * up * grad).astype(BF16)
                agb[m][y, k, 1, i] = (r * r * grad).astype(BF16)
                return 0

            lax.fori_loop(0, HALF, body, 0, unroll=True)
            spread("g", agb[m], m, grad_sems)

        def spread_hidden(m):
            spread("h", agh[m], m, hid_sems)

        def forward_grads(m):
            forward("g", agb[m], m, grad_sems)

        def expand(m, sources, targets):
            def body(n, _):
                cut = pl.ds(pl.multiple_of(n * 128, 128), 128)
                for tb in range(2):
                    ya, ia = inv_y[m, tb, 2 * n], inv_i[m, tb, 2 * n]
                    yb, ib = inv_y[m, tb, 2 * n + 1], inv_i[m, tb, 2 * n + 1]
                    for kk in range(2):
                        for src, dst in zip(sources, targets):
                            a = src(ya, kk, ia).astype(F32)
                            b = src(yb, kk, ib).astype(F32)
                            top = 64 * tb + 16 * kk
                            dst[m, top : top + 16, cut] = jnp.where(left16, a, pltpu.roll(b, 64, 1)).astype(BF16)
                            dst[m, top + 32 : top + 48, cut] = jnp.where(left16, pltpu.roll(a, 64, 1), b).astype(BF16)
                return 0

            lax.fori_loop(0, NBLK // 2, body, 0, unroll=True)

        def expand_grads(m):
            for d in (0, 1, 3, 2):
                arrived("gp", m, d)
            expand(
                m, (lambda a, b, c: agb[m][a, b, 0, c], lambda a, b, c: agb[m][a, b, 1, c]), (gh, gu)
            )
            start_local((3, m), gh.at[m], gh_hbm.at[m], out_sem.at[3, m])
            start_local((4, m), gu.at[m], gu_hbm.at[m], out_sem.at[4, m])

        def input_grad(m):
            def body(j, half):
                cut = pl.ds(pl.multiple_of(j * 256, 256), 256)
                rows = pl.ds(pl.multiple_of(half * 512 + j * 256, 256), 256)
                part = jnp.dot(gh[m], wgt[:, rows], preferred_element_type=F32)
                part = part + jnp.dot(gu[m], wut[:, rows], preferred_element_type=F32)
                dxf[m, half, :, cut] = part
                dxs[m, half, :, cut] = part.astype(BF16)

            for half in range(2):
                lax.fori_loop(0, 2, lambda j, c: (body(j, half), c)[1], 0, unroll=True)
                for i in far_first:
                    start(
                        ("rs", m, half, i), dxs.at[m, half, rows16(at_col(COL_STEPS[i]))], rr.at[m, half, i],
                        rs_s.at[m, half, i], rs_r.at[m, half, i], col_dev(COL_STEPS[i]), rr.at[m, half, i],
                    )

        def finish(m):
            for half in range(2):
                cols = slice(512 * half, 512 * half + 512)
                for i in range(7):
                    arrived("rs", m, half, i)
                total = dys[m, rows16(col), cols].astype(F32) + dxf[m, half, rows16(col), :]
                for i in range(7):
                    total = total + rr[m, half, i].astype(F32)
                sent_ref[0, m, :, cols] = total.astype(BF16)
                if is_last:
                    start(
                        ("hand", m, half), sent_ref.at[0, m, :, halves[half]], dys.at[m, rows16(col), halves[half]],
                        hand_s.at[m, half], hand_r.at[m, half], relay,
                    )

        def turn():
            for i, (src, dst) in enumerate(((wg, wgt), (wu, wut))):
                local.pop(("w", i)).wait()

                def body(j, _):
                    cut = pl.ds(pl.multiple_of(j * 256, 256), 256)
                    dst[cut, :] = src[:, cut].T
                    return 0

                lax.fori_loop(0, 7, body, 0)
            local.pop(("w", 2)).wait()

            def body(j, _):
                cut = pl.ds(pl.multiple_of(j * 256, 256), 256)
                wdt[:, cut] = wd[cut, :].T
                return 0

            lax.fori_loop(0, 7, body, 0)

        def turn_x():
            for m in range(2):
                xt[:, TOK * m : TOK * m + TOK] = xs[m].T
            start_local((0, 0), xt, xt_hbm, out_sem.at[0, 0])

        def hidden(m):
            forward("h", agh[m], m, hid_sems)
            for d in range(4):
                arrived("hp", m, d)
            expand(m, (lambda a, b, c: agh[m][a, b, c],), (hid,))
            start_local((2, m), hid.at[m], hid_hbm.at[m], out_sem.at[2, m])

        def drain():
            for key in [key for key in sends if key[:2] != ("rs", 1)]:
                sends.pop(key).wait_send()
            for key in list(local):
                local.pop(key).wait()

        for m in expected:
            for half in range(2):
                block = dys.at[m, rows16(dy_block(col)), halves[half]]
                recvs["hand", m, half] = remote(block, block, hand_s.at[m, half], hand_r.at[m, half], relay)
        table = dict(
            ax=spread_x, ady=spread_top, wx=wait_x, inv=invert, turn=turn, gu=gate_up, gs=gate_sums, hs=spread_hidden, xt=turn_x, drain=drain, bk=back, rp=reduce_pair, act=activate, fwd=forward_grads, ex=expand_grads,
            dx=input_grad, fin=finish, hid=hidden, dy=take_dy,
        )
        for name, *where in plan:
            table[name](*where)
        for c in sends.values():
            c.wait_send()
        for c in recvs.values():
            c.wait_recv()
        for c in local.values():
            c.wait()

    plan0, plan1 = plans
    handed = tuple(m for m in range(2) if ("fin", m) in plan1)

    @pl.when(last)
    def _():
        run(True, plan1, ())

    @pl.when(sec == 0)
    def _():
        run(False, plan0, handed)


PLAN1 = (
    ("ax", 0), ("inv",), ("ady", 0), ("turn",), ("wx", 0), ("ax", 1), ("ady", 1), ("gu", 0), ("bk", 0), ("rp", 0, 0),
    ("rp", 0, 1), ("wx", 1), ("gu", 1), ("gs", 0), ("rp", 1, 0), ("bk", 1), ("act", 0), ("rp", 1, 1), ("fwd", 0),
    ("ex", 0), ("gs", 1), ("act", 1), ("dx", 0), ("fwd", 1), ("ex", 1), ("fin", 0), ("dx", 1), ("fin", 1),
    ("hs", 0), ("hs", 1), ("xt",), ("hid", 0), ("hid", 1),
)
PLAN0 = (
    ("ax", 0), ("ax", 1), ("inv",), ("turn",), ("wx", 0), ("gu", 0), ("wx", 1), ("gu", 1), ("rp", 0, 0), ("rp", 1, 0),
    ("gs", 0), ("hs", 0), ("gs", 1), ("hs", 1), ("xt",), ("hid", 0), ("hid", 1), ("dy", 0), ("bk", 0), ("rp", 0, 1),
    ("dy", 1), ("act", 0), ("bk", 1), ("rp", 1, 1), ("fwd", 0), ("ex", 0), ("act", 1), ("dx", 0), ("fwd", 1),
    ("ex", 1), ("fin", 0), ("dx", 1), ("drain",), ("fin", 1),
)


def relay_call(layer_input, top_grad, gate_weight, up_weight, down_weight, activity, plans=(PLAN0, PLAN1), number=1):
    any_space = pl.BlockSpec(memory_space=pl.ANY)
    hbm = pl.BlockSpec(memory_space=pltpu.HBM)
    dma = pltpu.SemaphoreType.DMA
    vm = pltpu.VMEM
    tile = (HALF, 16, 128)
    return pl.pallas_call(
        functools.partial(relay_kernel, plans),
        name="relay",
        out_shape=(
            jax.ShapeDtypeStruct((1, 2, 16, DL), BF16),
            jax.ShapeDtypeStruct((DL, 2 * TOK), BF16),
            jax.ShapeDtypeStruct((2, TOK, DL), BF16),
            jax.ShapeDtypeStruct((2, TOK, FL), BF16),
            jax.ShapeDtypeStruct((2, TOK, FL), BF16),
            jax.ShapeDtypeStruct((2, TOK, FL), BF16),
        ),
        in_specs=[hbm] * 6,
        out_specs=(pl.BlockSpec(memory_space=pltpu.VMEM),) + (any_space,) * 5,
        scratch_shapes=[
            vm((2, TOK, DL), BF16), vm((DL, 2 * TOK), BF16), vm((2, TOK, DL), BF16),
            vm((DL, FL), BF16), vm((DL, FL), BF16), vm((FL, DL), BF16),
            vm((FL, DL), BF16), vm((FL, DL), BF16), vm((DL, FL), BF16),
            vm((2, 3, 2, NBLK, 32, 128), F32),
            vm((2, 3, 4) + tile, F32), vm((2, 3, 4) + tile, F32),
            vm((2, 3) + tile, F32), vm((2, 3, 3) + tile, BF16), vm((2, 3, 3) + tile, BF16),
            vm((5, 2, 2) + tile, BF16), vm((5, 2, 2) + tile, BF16),
            vm((5, 2) + tile, BF16), vm((5, 2) + tile, BF16),
            vm((2, TOK, FL), BF16), vm((2, TOK, FL), BF16), vm((2, TOK, FL), BF16),
            vm((2, 2, TOK, DL // 2), F32), vm((2, 2, TOK, DL // 2), BF16), vm((2, 2, 7, 16, DL // 2), BF16),
            pltpu.SMEM((1, 2, 2, 1, SLOTS), jnp.int32),
            pltpu.SMEM((2, 2, NBLK), jnp.int32), pltpu.SMEM((2, 2, NBLK), jnp.int32),
            dma((3,)), dma((5,)), dma((6, 2)),
            dma((2, 7)), dma((2, 7)), dma((2, 2, 7)), dma((2, 2, 7)),
            dma((2, 2)), dma((2, 2)), dma((2, 2, 3)), dma((2, 2, 3)),
            dma((2, 3)), dma((2, 3)), dma((2, 4)), dma((2, 4)),
            dma((2, 3)), dma((2, 3)), dma((2, 4)), dma((2, 4)),
            dma((2, 2, 7)), dma((2, 2, 7)), dma((2, 2)), dma((2, 2)),
        ],
        compiler_params=pltpu.CompilerParams(
            collective_id=number, has_side_effects=True, vmem_limit_bytes=48 * 2**20
        ),
        cost_estimate=pl.CostEstimate(flops=5 * 2**30, bytes_accessed=16 * 2**20, transcendentals=0),
    )(*(
        pltpu.with_memory_space_constraint(a, pltpu.HBM)
        for a in (layer_input, top_grad, gate_weight, up_weight, down_weight, activity)
    ))


def weights_kernel(xt_ref, dy_ref, hid_ref, gh_ref, gu_ref, sent_ref, out_sent, og, ou, od):
    @pl.when(pl.program_id(0) == 0)
    def _():
        out_sent[...] = sent_ref[...]

    cut = pl.ds(pl.multiple_of(pl.program_id(0) * 256, 256), 256)
    og[0] = jnp.dot(xt_ref[cut, :], gh_ref[...], preferred_element_type=F32).astype(BF16)
    ou[0] = jnp.dot(xt_ref[cut, :], gu_ref[...], preferred_element_type=F32).astype(BF16)
    od[0] = lax.dot_general(hid_ref[...], dy_ref[:, cut], TN, preferred_element_type=F32).astype(BF16)


def weights_call(xt, dy_all, hid, gh, gu, sent):
    whole = lambda shape: pl.BlockSpec(shape, lambda j: (0,) * len(shape))
    return pl.pallas_call(
        weights_kernel,
        name="weight_grads",
        grid=(DL // 256,),
        out_shape=(
            jax.ShapeDtypeStruct((1, 2, 16, DL), BF16),
            jax.ShapeDtypeStruct((1, DL, FL), BF16),
            jax.ShapeDtypeStruct((1, DL, FL), BF16),
            jax.ShapeDtypeStruct((1, FL, DL), BF16),
        ),
        in_specs=[pl.BlockSpec(memory_space=pltpu.VMEM)] * 6,
        out_specs=(
            whole((1, 2, 16, DL)),
            pl.BlockSpec((1, 256, FL), lambda j: (0, j, 0)),
            pl.BlockSpec((1, 256, FL), lambda j: (0, j, 0)),
            pl.BlockSpec((1, FL, 256), lambda j: (0, 0, j)),
        ),
        compiler_params=pltpu.CompilerParams(
            dimension_semantics=("arbitrary",), vmem_limit_bytes=24 * 2**20
        ),
    )(xt, dy_all, hid, gh, gu, sent)


def shards(layer_input, top_grad, gate_weight, up_weight, down_weight, activity):
    sent, xt, dy_all, hid, gh, gu = relay_call(
        layer_input, top_grad, gate_weight, up_weight, down_weight, activity
    )
    flat = lambda a: a.reshape(2 * TOK, a.shape[-1])
    return weights_call(xt, flat(dy_all), flat(hid), flat(gh), flat(gu), sent)


def solution(mesh):
    in_specs = (
        P("section", None, "col", "row"),
        P(None, "col", "row"),
        P("section", "row", "col"),
        P("section", "row", "col"),
        P("section", "col", "row"),
        P("section", None, None, "col", None),
    )
    out_specs = (
        P("section", None, "col", "row"),
        P("section", "row", "col"),
        P("section", "row", "col"),
        P("section", "col", "row"),
    )
    return jax.shard_map(shards, mesh=mesh, in_specs=in_specs, out_specs=out_specs, check_vma=False)
```

```python
import functools

import jax
import jax.numpy as jnp
from jax import lax
from jax.experimental import pallas as pl
from jax.experimental.pallas import tpu as pltpu
from jax.sharding import PartitionSpec as P

MESH = pl.DeviceIdType.MESH
F32, BF16 = jnp.float32, jnp.bfloat16
NT = (((1,), (1,)), ((), ()))

BLK = 64
TOK = 128
DL = 1024
FL = 1792
NBLK = 28
SLOTS = 14
HALF = 7
COL_STEPS = ((1, 0), (3, 0), (2, 0), (0, 1), (1, 1), (3, 1), (2, 1))


def relay_kernel(
    plans,
    x_hbm, top_hbm, wg_hbm, wu_hbm, wd_hbm, act_hbm,
    sent_ref, xt_hbm, dyall_hbm, hid_hbm, gh_hbm, gu_hbm,
    xs, xt, dys, wg, wu, wd, wgt, wut, wdt, dn, ps, pr, yo, ys, yr,
    agb0, agb1, agh0, agh1, hid, hidt, gh, gu, dxf, dxs, rr, act_ref, inv_y, inv_i,
    w_sem, own_sem, out_sem,
    x_s, x_r, dy_s, dy_r, pair_s, pair_r, y_s, y_r,
    ag_s, ag_r, agp_s, agp_r, hg_s, hg_r, hgp_s, hgp_r, rs_s, rs_r, hand_s, hand_r,
):
    agb, agh = (agb0, agb1), (agh0, agh1)
    sec, row, col = (lax.axis_index(a) for a in ("section", "row", "col"))
    y, k = row // 2, lax.rem(row, 2)
    z, xl = col // 2, lax.rem(col, 2)
    last = sec == 1

    def at_col(step, sign=1):
        dz, dx = step
        zz = lax.rem(z + (dz if sign > 0 else 4 - dz), 4)
        return zz * 2 + ((1 - xl) if dx else xl)

    def col_dev(step, sign=1):
        return (sec, row, at_col(step, sign))

    def y_at(d):
        return lax.rem(y + d, 4)

    def y_dev(d):
        return (sec, y_at(d) * 2 + k, col)

    pair = (sec, 2 * y + 1 - k, col)
    relay = (1 - sec, row, 2 * z + 1 - xl)

    def remote(src, dst, ss, rs, dev):
        return pltpu.make_async_remote_copy(
            src_ref=src, dst_ref=dst, send_sem=ss, recv_sem=rs, device_id=dev, device_id_type=MESH
        )

    def rows16(c):
        return pl.ds(pl.multiple_of(c * 16, 16), 16)

    lists = pltpu.make_async_copy(act_hbm, act_ref, own_sem.at[4])
    weights = [
        pltpu.make_async_copy(src.at[0], dst, w_sem.at[i])
        for i, (src, dst) in enumerate(((wg_hbm, wg), (wu_hbm, wu), (wd_hbm, wd)))
    ]
    own_x = [
        pltpu.make_async_copy(x_hbm.at[0, m], xs.at[m, rows16(col)], own_sem.at[m]) for m in range(2)
    ]
    own_dy = [
        pltpu.make_async_copy(top_hbm.at[m], dys.at[m, rows16(col)], own_sem.at[2 + m])
        for m in range(2)
    ]
    lists.start()
    for c in own_x:
        c.start()
    for c in weights:
        c.start()

    barrier = pltpu.get_barrier_semaphore()
    partners = [col_dev(s) for s in COL_STEPS] + [y_dev(d) for d in (1, 2, 3)] + [pair, relay]
    for dev in partners:
        pl.semaphore_signal(barrier, inc=1, device_id=dev, device_id_type=MESH)
    pl.semaphore_wait(barrier, len(partners))

    def invert():
        lists.wait()
        for m in range(2):
            agb[m][4] = jnp.zeros(agb[m].shape[1:], BF16)
            agh[m][4] = jnp.zeros(agh[m].shape[1:], BF16)
            for tb in range(2):
                def body(n, _):
                    slot = jnp.int32(2 * SLOTS)
                    for s in range(SLOTS):
                        slot = jnp.where(act_ref[0, m, tb, 0, s] == n, s, slot)
                    inv_y[m, tb, n] = jnp.where(slot < SLOTS, 2 * tb + jnp.where(slot < HALF, 0, 1), 4)
                    inv_i[m, tb, n] = jnp.where(
                        slot < SLOTS, jnp.where(slot < HALF, slot, slot - HALF), 0
                    )
                    return 0

                lax.fori_loop(0, NBLK, body, 0)

    left = lax.broadcasted_iota(jnp.int32, (32, 128), 1) < 64
    left16 = lax.broadcasted_iota(jnp.int32, (16, 128), 1) < 64
    MATS = ((0, 2), (2, 1))
    far_first = (6, 4, 5, 2, 3, 0, 1)
    halves = (pl.ds(0, DL // 2), pl.ds(DL // 2, DL // 2))

    def run(is_last, plan, expected):
        sends, recvs, local = {}, {}, {}

        def start(key, src, dst, ss, rs, dev, landing=None):
            c = remote(src, dst, ss, rs, dev)
            c.start()
            sends[key] = c
            if landing is not None:
                recvs[key] = remote(landing, landing, ss, rs, dev)

        def arrived(*key):
            recvs.pop(key).wait_recv()

        local.update({("w", i): c for i, c in enumerate(weights)})
        local.update({("x", m): c for m, c in enumerate(own_x)})

        def start_local(key, src, dst, sem):
            c = pltpu.make_async_copy(src, dst, sem)
            c.start()
            local[key] = c

        def dy_block(c):
            return c if is_last else c + 1 - 2 * lax.rem(c, 2)

        def lay_out(acc, m, mat, j):
            for tb in range(2):
                for h in range(2):
                    lo = acc[64 * tb : 64 * tb + 32, 128 * h : 128 * h + 128]
                    hi = acc[64 * tb + 32 : 64 * tb + 64, 128 * h : 128 * h + 128]
                    dn[m, mat, tb, 4 * j + 2 * h] = jnp.where(left, lo, pltpu.roll(hi, 64, 1))
                    dn[m, mat, tb, 4 * j + 2 * h + 1] = jnp.where(left, pltpu.roll(lo, 64, 1), hi)

        def send_pair(m, j):
            lo, n = MATS[j]
            far = pl.ds(pl.multiple_of(16 * (1 - k), 16), 16)

            def body(i, _):
                for yy in range(4):
                    tb, sh = yy // 2, yy % 2
                    b = jnp.minimum(act_ref[0, m, tb, 0, sh * HALF + i], NBLK - 1)
                    for mat in range(lo, lo + n):
                        ps[m, mat, yy, i] = dn[m, mat, tb, b, far, :]
                return 0

            lax.fori_loop(0, HALF, body, 0, unroll=True)
            cut = pl.ds(lo, n)
            start(
                ("pair", m, j), ps.at[m, cut], pr.at[m, cut], pair_s.at[m, j], pair_r.at[m, j], pair,
                pr.at[m, cut],
            )

        def spread_x(m):
            for i in far_first:
                step = COL_STEPS[i]
                start(
                    ("x", m, i), x_hbm.at[0, m], xs.at[m, rows16(col)], x_s.at[m, i], x_r.at[m, i],
                    col_dev(step), xs.at[m, rows16(at_col(step, -1))],
                )

        def spread_top(m):
            own_dy[m].start()
            local["dy", m] = own_dy[m]
            for half in range(2):
                spread_dy(m, half, top_hbm.at[m, :, halves[half]])

        def wait_x(m):
            local.pop(("x", m)).wait()
            for i in range(7):
                arrived("x", m, i)

        def spread_dy(m, half, src):
            block = rows16(dy_block(col))
            cols = halves[half]
            for i in far_first:
                step = COL_STEPS[i]
                start(
                    ("dy", m, half, i), src, dys.at[m, block, cols], dy_s.at[m, half, i], dy_r.at[m, half, i],
                    col_dev(step), dys.at[m, rows16(dy_block(at_col(step, -1))), cols],
                )

        def take_dy(m):
            for half in range(2):
                arrived("hand", m, half)
                spread_dy(m, half, dys.at[m, rows16(dy_block(col)), halves[half]])

        def gate_up(m):
            def body(j, _):
                cut = pl.ds(pl.multiple_of(j * 256, 256), 256)
                lay_out(jnp.dot(xs[m], wg[:, cut], preferred_element_type=F32), m, 0, j)
                lay_out(jnp.dot(xs[m], wu[:, cut], preferred_element_type=F32), m, 1, j)
                return 0

            lax.fori_loop(0, 7, body, 0, unroll=True)
            send_pair(m, 0)

        def back(m):
            if is_last:
                local.pop(("dy", m)).wait()
            for half in range(2):
                for i in range(7):
                    arrived("dy", m, half, i)
            start_local((1, m), dys.at[m], dyall_hbm.at[m], out_sem.at[1, m])

            def body(j, _):
                cut = pl.ds(pl.multiple_of(j * 256, 256), 256)
                grad = jnp.dot(dys[m], wdt[:, cut], preferred_element_type=F32)
                lay_out(grad, m, 2, j)
                return 0

            lax.fori_loop(0, 7, body, 0, unroll=True)
            send_pair(m, 1)

        def reduce_pair(m, j):
            arrived("pair", m, j)
            lo, n = MATS[j]
            near = pl.ds(pl.multiple_of(16 * k, 16), 16)
            cut = pl.ds(lo, n)
            for d in (2, 1, 3, 0):
                yy = y_at(d)
                tb, sh = yy // 2, lax.rem(yy, 2)

                def body(i, _):
                    b = jnp.minimum(act_ref[0, m, tb, 0, sh * HALF + i], NBLK - 1)
                    for mat in range(lo, lo + n):
                        total = dn[m, mat, tb, b, near, :] + pr[m, mat, yy, i]
                        if d:
                            ys[m, d - 1, mat, i] = total.astype(BF16)
                        else:
                            yo[m, mat, i] = total
                    return 0

                lax.fori_loop(0, HALF, body, 0, unroll=True)
                if d:
                    start(
                        ("y", m, j, d), ys.at[m, d - 1, cut], yr.at[m, d - 1, cut],
                        y_s.at[m, j, d - 1], y_r.at[m, j, d - 1], y_dev(d), yr.at[m, d - 1, cut],
                    )

        def spread(name, buf, m, sems):
            ss, rs, pss, prs = sems
            for d in (2, 1, 3):
                start(
                    (name, m, d), buf.at[y, k], buf.at[y, k], ss.at[m, d - 1], rs.at[m, d - 1], y_dev(d),
                    buf.at[y_at(4 - d), k],
                )
            start((name + "p", m, 0), buf.at[y, k], buf.at[y, k], pss.at[m, 0], prs.at[m, 0], pair, buf.at[y, 1 - k])

        def forward(name, buf, m, sems):
            ss, rs, pss, prs = sems
            for d in (1, 3, 2):
                arrived(name, m, d)
                yy = y_at(4 - d)
                start(
                    (name + "p", m, d), buf.at[yy, k], buf.at[yy, k], pss.at[m, d], prs.at[m, d], pair,
                    buf.at[yy, 1 - k],
                )

        grad_sems, hid_sems = (ag_s, ag_r, agp_s, agp_r), (hg_s, hg_r, hgp_s, hgp_r)

        def total(m, mat, i):
            value = yo[m, mat, i]
            for d in range(3):
                value = value + yr[m, d, mat, i].astype(F32)
            return value

        def gate_sums(m):
            for d in (1, 2, 3):
                arrived("y", m, 0, d)

            def body(i, _):
                r = jnp.maximum(total(m, 0, i), 0.0)
                up = total(m, 1, i)
                yo[m, 0, i] = r
                yo[m, 1, i] = up
                agh[m][y, k, i] = (r * r * up).astype(BF16)
                return 0

            lax.fori_loop(0, HALF, body, 0, unroll=True)

        def activate(m):
            for d in (1, 2, 3):
                arrived("y", m, 1, d)

            def body(i, _):
                r, up, grad = yo[m, 0, i], yo[m, 1, i], total(m, 2, i)
                agb[m][y, k, 0, i] = (2.0 * r * up * grad).astype(BF16)
                agb[m][y, k, 1, i] = (r * r * grad).astype(BF16)
                return 0

            lax.fori_loop(0, HALF, body, 0, unroll=True)
            spread("g", agb[m], m, grad_sems)

        def spread_hidden(m):
            spread("h", agh[m], m, hid_sems)

        def forward_grads(m):
            forward("g", agb[m], m, grad_sems)

        def expand(m, sources, targets):
            def body(n, _):
                cut = pl.ds(pl.multiple_of(n * 128, 128), 128)
                for tb in range(2):
                    ya, ia = inv_y[m, tb, 2 * n], inv_i[m, tb, 2 * n]
                    yb, ib = inv_y[m, tb, 2 * n + 1], inv_i[m, tb, 2 * n + 1]
                    for kk in range(2):
                        for src, dst in zip(sources, targets):
                            a = src(ya, kk, ia).astype(F32)
                            b = src(yb, kk, ib).astype(F32)
                            top = 64 * tb + 16 * kk
                            dst[m, top : top + 16, cut] = jnp.where(left16, a, pltpu.roll(b, 64, 1)).astype(BF16)
                            dst[m, top + 32 : top + 48, cut] = jnp.where(left16, pltpu.roll(a, 64, 1), b).astype(BF16)
                return 0

            lax.fori_loop(0, NBLK // 2, body, 0, unroll=True)

        def expand_grads(m):
            for d in (0, 1, 3, 2):
                arrived("gp", m, d)
            expand(
                m, (lambda a, b, c: agb[m][a, b, 0, c], lambda a, b, c: agb[m][a, b, 1, c]), (gh, gu)
            )
            start_local((3, m), gh.at[m], gh_hbm.at[m], out_sem.at[3, m])
            start_local((4, m), gu.at[m], gu_hbm.at[m], out_sem.at[4, m])

        def input_grad(m):
            def body(j, half):
                cut = pl.ds(pl.multiple_of(j * 256, 256), 256)
                rows = pl.ds(pl.multiple_of(half * 512 + j * 256, 256), 256)
                part = jnp.dot(gh[m], wgt[:, rows], preferred_element_type=F32)
                part = part + jnp.dot(gu[m], wut[:, rows], preferred_element_type=F32)
                dxf[m, half, :, cut] = part
                dxs[m, half, :, cut] = part.astype(BF16)

            for half in range(2):
                lax.fori_loop(0, 2, lambda j, c: (body(j, half), c)[1], 0, unroll=True)
                for i in far_first:
                    start(
                        ("rs", m, half, i), dxs.at[m, half, rows16(at_col(COL_STEPS[i]))], rr.at[m, half, i],
                        rs_s.at[m, half, i], rs_r.at[m, half, i], col_dev(COL_STEPS[i]), rr.at[m, half, i],
                    )

        def finish(m):
            for half in range(2):
                cols = slice(512 * half, 512 * half + 512)
                for i in range(7):
                    arrived("rs", m, half, i)
                total = dys[m, rows16(col), cols].astype(F32) + dxf[m, half, rows16(col), :]
                for i in range(7):
                    total = total + rr[m, half, i].astype(F32)
                sent_ref[0, m, :, cols] = total.astype(BF16)
                if is_last:
                    start(
                        ("hand", m, half), sent_ref.at[0, m, :, halves[half]], dys.at[m, rows16(col), halves[half]],
                        hand_s.at[m, half], hand_r.at[m, half], relay,
                    )

        def turn():
            for i, (src, dst) in enumerate(((wg, wgt), (wu, wut))):
                local.pop(("w", i)).wait()

                def body(j, _):
                    cut = pl.ds(pl.multiple_of(j * 256, 256), 256)
                    dst[cut, :] = src[:, cut].T
                    return 0

                lax.fori_loop(0, 7, body, 0)
            local.pop(("w", 2)).wait()

            def body(j, _):
                cut = pl.ds(pl.multiple_of(j * 256, 256), 256)
                wdt[:, cut] = wd[cut, :].T
                return 0

            lax.fori_loop(0, 7, body, 0)

        def turn_x():
            for m in range(2):
                xt[:, TOK * m : TOK * m + TOK] = xs[m].T
            start_local((0, 0), xt, xt_hbm, out_sem.at[0, 0])

        def hidden(m):
            forward("h", agh[m], m, hid_sems)
            for d in range(4):
                arrived("hp", m, d)
            expand(m, (lambda a, b, c: agh[m][a, b, c],), (hid,))
            hidt[:, TOK * m : TOK * m + TOK] = hid[m].T
            if m == 1:
                start_local((2, 0), hidt, hid_hbm, out_sem.at[2, 0])

        def drain():
            for key in [key for key in sends if key[:2] != ("rs", 1)]:
                sends.pop(key).wait_send()
            for key in list(local):
                local.pop(key).wait()

        for m in expected:
            for half in range(2):
                block = dys.at[m, rows16(dy_block(col)), halves[half]]
                recvs["hand", m, half] = remote(block, block, hand_s.at[m, half], hand_r.at[m, half], relay)
        table = dict(
            ax=spread_x, ady=spread_top, wx=wait_x, inv=invert, turn=turn, gu=gate_up, gs=gate_sums, hs=spread_hidden, xt=turn_x, drain=drain, bk=back, rp=reduce_pair, act=activate, fwd=forward_grads, ex=expand_grads,
            dx=input_grad, fin=finish, hid=hidden, dy=take_dy,
        )
        for name, *where in plan:
            table[name](*where)
        for c in sends.values():
            c.wait_send()
        for c in recvs.values():
            c.wait_recv()
        for c in local.values():
            c.wait()

    plan0, plan1 = plans
    handed = tuple(m for m in range(2) if ("fin", m) in plan1)

    @pl.when(last)
    def _():
        run(True, plan1, ())

    @pl.when(sec == 0)
    def _():
        run(False, plan0, handed)


PLAN1 = (
    ("ax", 0), ("inv",), ("ady", 0), ("turn",), ("wx", 0), ("ax", 1), ("ady", 1), ("gu", 0), ("bk", 0), ("rp", 0, 0),
    ("rp", 0, 1), ("wx", 1), ("gu", 1), ("gs", 0), ("rp", 1, 0), ("bk", 1), ("act", 0), ("rp", 1, 1), ("fwd", 0),
    ("ex", 0), ("gs", 1), ("act", 1), ("dx", 0), ("fwd", 1), ("ex", 1), ("fin", 0), ("dx", 1), ("fin", 1),
    ("hs", 0), ("hs", 1), ("xt",), ("hid", 0), ("hid", 1),
)
PLAN0 = (
    ("ax", 0), ("ax", 1), ("inv",), ("turn",), ("wx", 0), ("gu", 0), ("wx", 1), ("gu", 1), ("rp", 0, 0), ("rp", 1, 0),
    ("gs", 0), ("hs", 0), ("gs", 1), ("hs", 1), ("xt",), ("hid", 0), ("hid", 1), ("dy", 0), ("bk", 0), ("rp", 0, 1),
    ("dy", 1), ("act", 0), ("bk", 1), ("rp", 1, 1), ("fwd", 0), ("ex", 0), ("act", 1), ("dx", 0), ("fwd", 1),
    ("ex", 1), ("fin", 0), ("dx", 1), ("drain",), ("fin", 1),
)


def relay_call(layer_input, top_grad, gate_weight, up_weight, down_weight, activity, plans=(PLAN0, PLAN1), number=1):
    any_space = pl.BlockSpec(memory_space=pl.ANY)
    hbm = pl.BlockSpec(memory_space=pltpu.HBM)
    dma = pltpu.SemaphoreType.DMA
    vm = pltpu.VMEM
    tile = (HALF, 16, 128)
    return pl.pallas_call(
        functools.partial(relay_kernel, plans),
        name="relay",
        out_shape=(
            jax.ShapeDtypeStruct((1, 2, 16, DL), BF16),
            jax.ShapeDtypeStruct((DL, 2 * TOK), BF16),
            jax.ShapeDtypeStruct((2, TOK, DL), BF16),
            jax.ShapeDtypeStruct((FL, 2 * TOK), BF16),
            jax.ShapeDtypeStruct((2, TOK, FL), BF16),
            jax.ShapeDtypeStruct((2, TOK, FL), BF16),
        ),
        in_specs=[hbm] * 6,
        out_specs=(pl.BlockSpec(memory_space=pltpu.VMEM),) + (any_space,) * 5,
        scratch_shapes=[
            vm((2, TOK, DL), BF16), vm((DL, 2 * TOK), BF16), vm((2, TOK, DL), BF16),
            vm((DL, FL), BF16), vm((DL, FL), BF16), vm((FL, DL), BF16),
            vm((FL, DL), BF16), vm((FL, DL), BF16), vm((DL, FL), BF16),
            vm((2, 3, 2, NBLK, 32, 128), F32),
            vm((2, 3, 4) + tile, F32), vm((2, 3, 4) + tile, F32),
            vm((2, 3) + tile, F32), vm((2, 3, 3) + tile, BF16), vm((2, 3, 3) + tile, BF16),
            vm((5, 2, 2) + tile, BF16), vm((5, 2, 2) + tile, BF16),
            vm((5, 2) + tile, BF16), vm((5, 2) + tile, BF16),
            vm((2, TOK, FL), BF16), vm((FL, 2 * TOK), BF16), vm((2, TOK, FL), BF16), vm((2, TOK, FL), BF16),
            vm((2, 2, TOK, DL // 2), F32), vm((2, 2, TOK, DL // 2), BF16), vm((2, 2, 7, 16, DL // 2), BF16),
            pltpu.SMEM((1, 2, 2, 1, SLOTS), jnp.int32),
            pltpu.SMEM((2, 2, NBLK), jnp.int32), pltpu.SMEM((2, 2, NBLK), jnp.int32),
            dma((3,)), dma((5,)), dma((6, 2)),
            dma((2, 7)), dma((2, 7)), dma((2, 2, 7)), dma((2, 2, 7)),
            dma((2, 2)), dma((2, 2)), dma((2, 2, 3)), dma((2, 2, 3)),
            dma((2, 3)), dma((2, 3)), dma((2, 4)), dma((2, 4)),
            dma((2, 3)), dma((2, 3)), dma((2, 4)), dma((2, 4)),
            dma((2, 2, 7)), dma((2, 2, 7)), dma((2, 2)), dma((2, 2)),
        ],
        compiler_params=pltpu.CompilerParams(
            collective_id=number, has_side_effects=True, vmem_limit_bytes=48 * 2**20
        ),
        cost_estimate=pl.CostEstimate(flops=5 * 2**30, bytes_accessed=16 * 2**20, transcendentals=0),
    )(*(
        pltpu.with_memory_space_constraint(a, pltpu.HBM)
        for a in (layer_input, top_grad, gate_weight, up_weight, down_weight, activity)
    ))


def weights_kernel(xt_ref, dy_ref, hid_ref, gh_ref, gu_ref, sent_ref, out_sent, og, ou, od):
    @pl.when(pl.program_id(0) == 0)
    def _():
        out_sent[...] = sent_ref[...]

    cut = pl.ds(pl.multiple_of(pl.program_id(0) * 256, 256), 256)
    og[0] = jnp.dot(xt_ref[cut, :], gh_ref[...], preferred_element_type=F32).astype(BF16)
    ou[0] = jnp.dot(xt_ref[cut, :], gu_ref[...], preferred_element_type=F32).astype(BF16)
    od[0] = jnp.dot(hid_ref[...], dy_ref[:, cut], preferred_element_type=F32).astype(BF16)


def weights_call(xt, dy_all, hid, gh, gu, sent):
    whole = lambda shape: pl.BlockSpec(shape, lambda j: (0,) * len(shape))
    return pl.pallas_call(
        weights_kernel,
        name="weight_grads",
        grid=(DL // 256,),
        out_shape=(
            jax.ShapeDtypeStruct((1, 2, 16, DL), BF16),
            jax.ShapeDtypeStruct((1, DL, FL), BF16),
            jax.ShapeDtypeStruct((1, DL, FL), BF16),
            jax.ShapeDtypeStruct((1, FL, DL), BF16),
        ),
        in_specs=[pl.BlockSpec(memory_space=pltpu.VMEM)] * 6,
        out_specs=(
            whole((1, 2, 16, DL)),
            pl.BlockSpec((1, 256, FL), lambda j: (0, j, 0)),
            pl.BlockSpec((1, 256, FL), lambda j: (0, j, 0)),
            pl.BlockSpec((1, FL, 256), lambda j: (0, 0, j)),
        ),
        compiler_params=pltpu.CompilerParams(
            dimension_semantics=("arbitrary",), vmem_limit_bytes=24 * 2**20
        ),
    )(xt, dy_all, hid, gh, gu, sent)


def shards(layer_input, top_grad, gate_weight, up_weight, down_weight, activity):
    sent, xt, dy_all, hid, gh, gu = relay_call(
        layer_input, top_grad, gate_weight, up_weight, down_weight, activity
    )
    flat = lambda a: a.reshape(2 * TOK, a.shape[-1])
    return weights_call(xt, flat(dy_all), hid, flat(gh), flat(gu), sent)


def solution(mesh):
    in_specs = (
        P("section", None, "col", "row"),
        P(None, "col", "row"),
        P("section", "row", "col"),
        P("section", "row", "col"),
        P("section", "col", "row"),
        P("section", None, None, "col", None),
    )
    out_specs = (
        P("section", None, "col", "row"),
        P("section", "row", "col"),
        P("section", "row", "col"),
        P("section", "col", "row"),
    )
    return jax.shard_map(shards, mesh=mesh, in_specs=in_specs, out_specs=out_specs, check_vma=False)
```
